512 devices in a mesh: dp: 4 (over x), expert: 16 (over z_hi, y, core), tensor: 8 (over z_lo).
Axes of the slice: x: 4, y: 4, z: 16 (z_hi: 2, z_lo: 8; z = z_hi * 8 + z_lo), core: 2. Of those that a mesh axis runs over, the one named last changes fastest.
Arguments:
- layer_grad: bfloat16 [8192, 4096], P(('dp', 'expert'), 'tensor'), may hold values from -6 to 6
- gate_probs: float32 [8192, 2], P(('dp', 'expert')), may hold values from 0.2 to 1
- expert_ids: int32 [8192, 2], P(('dp', 'expert')), may hold values from 0 to 15, all different within a row; in each aligned block of 128 rows (0 to 127, 128 to 255, ...) at most 20 rows name the same one
- down_weight: bfloat16 [16, 12288, 4096], P('expert', ('dp', 'tensor')), may hold values from -0.09375 to 0.09375
Outputs:
- hidden_grad: bfloat16 [16, 1280, 12288], P('expert', None, ('dp', 'tensor'))
The draws below stay inside these ranges and needn't reach their ends.
Inputs may be any that keep to these rules, and one draw needn't show every extreme that they name: `expert_ids`: within the rows of one token group (128 aligned rows) the two experts of a row differ, no expert is named more than 20 times, a bound that some block reaches.
All inputs are finite; a program needn't handle non-finite values.
Results may differ from the reference program's by a relative error of at most 0.0049.
Values may be sent and summed in bfloat16 or wider, within the bound.
A program may use at most 64 MiB of HBM per device.

```python
import math
import jax
import jax.numpy as jnp
import numpy as np
from jax import lax

D = 4096
EH = 12288
TOK_DEV = 128
EXPERTS = 16
CAP = 20
TOKENS = 8192


def block_levels(key, extent, cuts, low, top_value):
    level, own = 1.0, jax.random.fold_in(key, 6)
    for axis_at, parts in cuts:
        heights = jnp.exp(jax.random.uniform(jax.random.fold_in(own, axis_at), (parts,), jnp.float32, low / len(cuts), top_value / len(cuts)))
        level = level * jnp.repeat(heights, extent[axis_at] // parts).reshape([-1 if axis == axis_at else 1 for axis in range(len(extent))])
    return level


def assign_block(key, own, number, rows, number_of, top, limit, slope):
    order = jax.random.permutation(key, number_of)
    heavy_load, usual = load_shares(number_of, rows * top, limit, slope, True), load_shares(number_of, rows * top, limit, slope, False)
    places = jnp.arange(number_of)

    def named(tallies, rotation):
        used = int((tallies > 0).sum())
        fixed = max(1, used // 4)
        moved = fixed + (places - fixed + rotation * (used - fixed)) % max(1, number_of - fixed)
        return jnp.zeros((number_of,), jnp.int32).at[order[jnp.where(places < fixed, places, moved)]].set(jnp.asarray(tallies, jnp.int32))

    tallies = jnp.where(number % 4 == 0, named(heavy_load, number // 4), named(usual, number - number // 4 - 1))
    mixed = jax.random.permutation(jax.random.fold_in(own, 3), number_of)
    source_of, receiver = mixed[0:number_of // 2 * 2:2], mixed[1:number_of // 2 * 2:2]
    margin = jnp.minimum(tallies[source_of] - 1, limit - tallies[receiver]) // 2
    margin = jnp.where((source_of == order[0]) | (receiver == order[0]) | (tallies[receiver] == 0), 0, jnp.maximum(margin, 0))
    moved = jax.random.randint(jax.random.fold_in(own, 4), (number_of // 2,), 0, 1 << 20) % (margin + 1)
    tallies = tallies.at[source_of].add(-moved).at[receiver].add(moved)
    members = jnp.searchsorted(jnp.cumsum(tallies), jnp.arange(rows * top), side="right").astype(jnp.int32)
    listing = members.reshape(top, rows).T
    listing = listing[jax.random.permutation(jax.random.fold_in(own, 1), rows)]
    rotation = jax.random.randint(jax.random.fold_in(own, 2), (rows, 1), 0, top)
    return jnp.take_along_axis(listing, (jnp.arange(top)[None, :] + rotation) % top, axis=1)


def load_shares(count, total, limit, lean, full):
    portions = [(1 << 20) // math.isqrt(standing ** lean) + 1 for standing in range(1, count + 1)]
    largest = limit if full else min(limit, max(-(-total // count), total * portions[0] // sum(portions)))
    least = 1 if total - largest >= count - 1 else 0
    counts, spare = [largest] + [least] * (count - 1), total - largest - least * (count - 1)
    while spare > 0:
        movable = [i for i in range(1, count) if counts[i] < largest] or [i for i in range(1, count) if counts[i] < limit]
        mass, budget = sum([portions[i] for i in movable]), spare
        for i in movable:
            extra = min(limit - counts[i], max(1, budget * portions[i] // mass), spare)
            counts[i] = counts[i] + extra
            spare = spare - extra
    return np.array(counts)


def scatter_about(own_key, dims, scale, most, cuts=(), kind=jnp.bfloat16):
    gain = block_levels(own_key, dims, cuts, -0.22, 0.18) if cuts else 1.0
    array = jax.random.normal(own_key, dims, jnp.float32) * scale * gain
    return jnp.minimum(jnp.maximum(array, -most), most).astype(kind)


def setup_inputs(seed: int = 0) -> dict:
    key_list = jax.random.split(jax.random.key(seed), 5)
    layer_grad = scatter_about(key_list[0], (TOKENS, D), 1.0, 6.0, ((0, 64), (1, 8)))
    gate_probs = jnp.clip(0.2 + 0.8 * jax.random.uniform(key_list[1], (TOKENS, 2), jnp.float32) ** block_levels(key_list[1], (TOKENS, 2), ((0, 64),), -0.2, 0.2), 0.2, 1.0)
    expert_ids_keys = jax.random.split(jax.random.fold_in(key_list[2], 1), TOKENS // TOK_DEV)
    expert_ids_turns = jax.random.permutation(jax.random.fold_in(key_list[2], 3), TOKENS // TOK_DEV)
    expert_ids = jax.vmap(lambda own, number: assign_block(jax.random.fold_in(key_list[2], 2), own, number, TOK_DEV, EXPERTS, 2, CAP, 2))(expert_ids_keys, expert_ids_turns).reshape((TOKENS, 2))
    down_weight = scatter_about(key_list[3], (EXPERTS, EH, D), D ** -0.5, 0.09375, ((0, 16), (1, 32)))
    return {"layer_grad": layer_grad, "gate_probs": gate_probs, "expert_ids": expert_ids, "down_weight": down_weight}


def reference(layer_grad, gate_probs, expert_ids, down_weight):
    groups = TOKENS // TOK_DEV
    flat = expert_ids.reshape(groups, 2 * TOK_DEV).astype(jnp.int32)
    onehot = (flat[:, :, None] == jnp.arange(EXPERTS, dtype=jnp.int32)[None, None, :]).astype(jnp.int32)
    ranks = jnp.sum((jnp.cumsum(onehot, axis=1) - onehot) * onehot, axis=2).astype(jnp.int32)
    places = (flat * CAP + ranks).reshape(groups, TOK_DEV, 2)
    slot_rows = jnp.arange(EXPERTS * CAP, dtype=jnp.int32)
    probs = gate_probs.reshape(groups, TOK_DEV, 2)
    mixing = jnp.zeros((groups, EXPERTS * CAP, TOK_DEV), jnp.float32)
    for choice_k in range(2):
        mixing = mixing + jnp.where(slot_rows[None, :, None] == places[:, None, :, choice_k], probs[:, None, :, choice_k], jnp.zeros((), jnp.float32))
    features = layer_grad.astype(jnp.float32).reshape(groups, TOK_DEV, D)
    routed = jnp.einsum("gst,gtd->gsd", mixing, features, precision=lax.Precision.HIGHEST).astype(jnp.bfloat16)
    routed = routed.reshape(groups, EXPERTS, CAP, D).transpose(1, 0, 2, 3).reshape(EXPERTS, groups * CAP, D)

    def expert_rows(pair):
        return jnp.dot(pair[0], pair[1].T, preferred_element_type=jnp.float32).astype(jnp.bfloat16)

    return lax.map(expert_rows, (routed, down_weight))
```

```python
import functools

import jax
import jax.numpy as jnp
from jax import lax
from jax.experimental import pallas as pl
from jax.experimental.pallas import tpu as pltpu
from jax.sharding import PartitionSpec as P

MESH = pl.DeviceIdType.MESH
MAIN = 16
TAIL = 4


def kernel(
    shape,
    feats, probs, ids, weight, out,
    routed, rows, passing, held_w, acc, acc_tail, w_sem,
    a_send, a_recv, z_send, z_recv, t_send, t_recv, x_send, x_recv, f_send, f_recv,
):
    dp, yc, zl, width = shape
    half = zl // 2
    ring = 2 * zl
    quarter = width // 4
    experts = 2 * yc
    x = lax.axis_index("dp")
    ex = lax.axis_index("expert")
    j = lax.axis_index("tensor")
    zh, c = ex // yc, ex % yc
    p = zh * zl + j

    def at_ring(pos):
        pos = (pos + ring) % ring
        return {"expert": (pos // zl) * yc + c, "tensor": pos % zl}

    def at_x(offset):
        return {"dp": (x + offset + dp) % dp}

    def at_c(offset):
        return {"expert": zh * yc + (c + offset) % yc}

    barrier = pltpu.get_barrier_semaphore()
    partners = [at_ring(p + 1), at_ring(p - 1), at_x(1), at_x(-1)] + [at_c(i) for i in range(1, yc)]
    for partner in partners:
        pl.semaphore_signal(barrier, inc=1, device_id=partner, device_id_type=MESH)

    w_copy = pltpu.make_async_copy(weight.at[0], held_w, w_sem)
    w_copy.start()

    tokens = feats.shape[0]
    who = [ids[k : k + 1, :] for k in range(2)]
    e_iota = lax.broadcasted_iota(jnp.int32, (experts, tokens), 0)
    named = [(e_iota == who[k]).astype(jnp.float32) for k in range(2)]
    before = lax.broadcasted_iota(jnp.int32, (tokens, tokens), 0) < lax.broadcasted_iota(jnp.int32, (tokens, tokens), 1)
    earlier = jnp.dot(
        (named[0] + named[1]).astype(jnp.bfloat16),
        jnp.where(before, 1.0, 0.0).astype(jnp.bfloat16),
        preferred_element_type=jnp.float32,
    )
    ranks = [
        jnp.sum(earlier * named[0], axis=0, keepdims=True).astype(jnp.int32),
        jnp.sum((earlier + named[0]) * named[1], axis=0, keepdims=True).astype(jnp.int32),
    ]
    row = lax.broadcasted_iota(jnp.int32, (experts * MAIN, tokens), 0)
    sub = lax.broadcasted_iota(jnp.int32, (experts * MAIN, quarter), 0) % MAIN // TAIL

    def gather(codes, wanted):
        hits = [codes[k] == wanted for k in range(2)]
        pick = jnp.where(hits[0] | hits[1], 1.0, 0.0).astype(jnp.bfloat16)
        scale = jnp.where(hits[0], probs[0:1, :], 0.0) + jnp.where(hits[1], probs[1:2, :], 0.0)
        scale = jnp.sum(scale, axis=1, keepdims=True)
        return jnp.dot(pick, feats[...], preferred_element_type=jnp.float32), scale

    got, scale = gather([jnp.where(ranks[k] < MAIN, who[k] * MAIN + ranks[k], -1) for k in range(2)], row)
    routed[:, :, 0:width] = (got * scale).astype(jnp.bfloat16).reshape(experts, MAIN, width)
    got, scale = gather(
        [jnp.where(ranks[k] >= MAIN, who[k] * TAIL + ranks[k] - MAIN, -1) for k in range(2)],
        row // MAIN * TAIL + row % TAIL,
    )
    tail = jnp.zeros((experts * MAIN, quarter), jnp.float32)
    for q in range(4):
        tail = tail + jnp.where(sub == q, got[:, q * quarter : (q + 1) * quarter], 0.0)
    routed[:, :, width : width + quarter] = (tail * scale).astype(jnp.bfloat16).reshape(experts, MAIN, quarter)

    pl.semaphore_wait(barrier, len(partners))

    def a_copy(i, other):
        target = (c + i) % yc
        source = routed.at[((1 - zh) if other else zh) * yc + target]
        return pltpu.make_async_remote_copy(
            src_ref=source,
            dst_ref=passing.at[j, c] if other else rows.at[p, x, c],
            send_sem=a_send.at[other, i],
            recv_sem=a_recv.at[other, i],
            device_id=at_c(i),
            device_id_type=MESH,
        )

    def a_arrived(i, other):
        origin = (c + yc - i) % yc
        place = passing.at[j, origin] if other else rows.at[p, x, origin]
        pltpu.make_async_copy(place, place, a_recv.at[other, i]).wait()

    for other in range(2):
        for i in range(1, yc):
            a_copy(i, other).start()
    rows[p, x, c] = routed[zh * yc + c]
    passing[j, c] = routed[(1 - zh) * yc + c]

    def unit_of(way, step):
        return (p + (step if way else -step) + ring) % ring

    def along(way):
        return zl - 1 - j if way else j

    def z_copy(way, step):
        place = rows.at[unit_of(way, step), x]
        return pltpu.make_async_remote_copy(
            src_ref=place,
            dst_ref=place,
            send_sem=z_send.at[way, step],
            recv_sem=z_recv.at[way, step + 1],
            device_id=at_ring(p + (-1 if way else 1)),
            device_id_type=MESH,
        )

    def z_arrived(way, step):
        place = rows.at[unit_of(way, step), x]
        pltpu.make_async_copy(place, place, z_recv.at[way, step]).wait()

    def t_place(way, step):
        return passing.at[(j + (step if way else -step) + zl) % zl]

    def t_copy(way, step, leaves):
        return pltpu.make_async_remote_copy(
            src_ref=t_place(way, step),
            dst_ref=rows.at[unit_of(way, step), x] if leaves else t_place(way, step),
            send_sem=t_send.at[way, step],
            recv_sem=(z_recv if leaves else t_recv).at[way, step + 1],
            device_id=at_ring(p + (-1 if way else 1)),
            device_id_type=MESH,
        )

    def t_arrived(way, step):
        place = t_place(way, step)
        pltpu.make_async_copy(place, place, t_recv.at[way, step]).wait()

    def z_forward(way, step):
        q = along(way)

        @pl.when((q < zl - 1) & (step <= q + half))
        def _():
            z_copy(way, step).start()

        @pl.when((q < zl - 1) & (step <= q - half))
        def _():
            t_copy(way, step, False).start()

        @pl.when((q == zl - 1) & (step <= q - half))
        def _():
            t_copy(way, step, True).start()

    def z_round(step):
        for way in range(2):
            q = along(way)

            @pl.when(step <= q + half)
            def _():
                z_arrived(way, step)

            @pl.when(step <= q - half)
            def _():
                t_arrived(way, step)

            z_forward(way, step)

    up, down = j + half, zl - 1 - j + half
    both = jnp.minimum(up, down)

    def unit_at(m):
        paired = m <= 2 * both
        step = jnp.where(paired, (m + 1) // 2, m - both)
        goes_up = jnp.where(paired, m % 2 == 1, up > down)
        return (p + jnp.where(goes_up, -step, step) + ring) % ring

    def x_copy(way, unit):
        place = rows.at[unit, x]
        return pltpu.make_async_remote_copy(
            src_ref=place,
            dst_ref=place,
            send_sem=x_send.at[way, unit],
            recv_sem=x_recv.at[way, unit],
            device_id=at_x(-1 if way else 1),
            device_id_type=MESH,
        )

    def x_arrived(way, unit):
        place = rows.at[unit, (x + (1 if way else dp - 1)) % dp]
        pltpu.make_async_copy(place, place, x_recv.at[way, unit]).wait()

    part = yc // 2

    def f_copy(way, unit):
        place = rows.at[unit, (x + (1 if way else dp - 1)) % dp, pl.ds(part * way, part)]
        return pltpu.make_async_remote_copy(
            src_ref=place,
            dst_ref=place,
            send_sem=f_send.at[way, unit],
            recv_sem=f_recv.at[way, unit],
            device_id=at_x(-1 if way else 1),
            device_id_type=MESH,
        )

    def f_arrived(way, unit):
        place = rows.at[unit, (x + 2) % dp, pl.ds(part * way, part)]
        pltpu.make_async_copy(place, place, f_recv.at[way, unit]).wait()

    def work(unit):
        for way in range(2):
            f_arrived(way, unit)
        zone = unit // zl
        cols = pl.ds(pl.multiple_of(unit % zl * width, width), width)
        w = held_w[:, cols]
        contract = (((1,), (1,)), ((), ()))
        count = dp * yc * MAIN
        whole = rows[unit, :, :, :, 0:width].reshape(count, width)
        acc[zone] += lax.dot_general(whole, w, contract, preferred_element_type=jnp.float32)
        quarters = rows[unit, :, :, :, width : width + quarter].reshape(count, quarter)
        of = lax.broadcasted_iota(jnp.int32, (count, quarter), 0) % MAIN // TAIL
        spread = jnp.concatenate(
            [jnp.where(of == q, quarters, jnp.zeros_like(quarters)) for q in range(4)], axis=1
        )
        acc_tail[zone] += lax.dot_general(spread, w, contract, preferred_element_type=jnp.float32)

    acc[...] = jnp.zeros_like(acc)
    acc_tail[...] = jnp.zeros_like(acc_tail)
    for i in range(1, yc):
        a_arrived(i, 0)
    for way in range(2):
        @pl.when(along(way) < zl - 1)
        def _():
            z_copy(way, 0).start()
    for way in range(2):
        x_copy(way, p).start()
    for i in range(1, yc):
        a_arrived(i, 1)
    for way in range(2):
        @pl.when((along(way) < zl - 1) & (along(way) >= half))
        def _():
            t_copy(way, 0, False).start()

        @pl.when(along(way) == zl - 1)
        def _():
            t_copy(way, 0, True).start()
    w_copy.wait()
    z_round(1)
    for way in range(2):
        x_copy(way, unit_at(1)).start()

    def turn(r, carry):
        @pl.when(r + 2 < ring)
        def _():
            for way in range(2):
                x_copy(way, unit_at(r + 2)).start()

        for way in range(2):
            x_arrived(way, unit_at(r))
            f_copy(way, unit_at(r)).start()
        z_round(r + 2)

        @pl.when(r >= 2)
        def _():
            work(unit_at(r - 2))

        return carry

    lax.fori_loop(0, ring, turn, 0)
    work(unit_at(ring - 2))
    work(unit_at(ring - 1))

    slots = MAIN + TAIL
    take = yc * MAIN
    out_row = lax.broadcasted_iota(jnp.int32, (yc * slots, yc * (MAIN + 8)), 0)
    in_row = lax.broadcasted_iota(jnp.int32, (yc * slots, yc * (MAIN + 8)), 1)
    group, slot = out_row // slots, out_row % slots
    source = jnp.where(slot < MAIN, group * MAIN + slot, take + group * 8 + slot - MAIN)
    place = jnp.where(source == in_row, 1.0, 0.0).astype(jnp.bfloat16)
    for zone in range(2):
        for at in range(dp):
            main = acc[zone, pl.ds(at * take, take), :].astype(jnp.bfloat16)
            ends = acc_tail[zone, pl.ds(at * take, take), :].reshape(yc, MAIN, acc.shape[-1])
            ends = ends[:, 0:8, :] + ends[:, 8:16, :]
            ends = ends.reshape(yc * 8, acc.shape[-1])
            turned = pltpu.roll(ends, yc * 8 - TAIL, 0)
            ends = (ends + turned).astype(jnp.bfloat16)
            done = jnp.dot(place, jnp.concatenate([main, ends], axis=0), preferred_element_type=jnp.float32)
            start = (at * 2 + zone) * yc * slots
            out[0, pl.ds(start, yc * slots), :] = done.astype(jnp.bfloat16)

    for other in range(2):
        for i in range(1, yc):
            a_copy(i, other).wait_send()

    def left(step, carry):
        for way in range(2):
            q = along(way)

            @pl.when((q < zl - 1) & (step <= q + half))
            def _():
                z_copy(way, step).wait_send()

            @pl.when(step <= q - half)
            def _():
                t_copy(way, step, False).wait_send()

            x_copy(way, step).wait_send()
            f_copy(way, step).wait_send()
        return carry

    lax.fori_loop(0, ring, left, 0)


def body(layer_grad, gate_probs, expert_ids, down_weight):
    dp, zl = lax.axis_size("dp"), lax.axis_size("tensor")
    experts = down_weight.shape[0] * lax.axis_size("expert")
    yc = experts // 2
    ring = 2 * zl
    width = layer_grad.shape[1]
    hidden = down_weight.shape[1]
    half = zl // 2
    chunk = (MAIN, width + width // 4)
    count = dp * yc * MAIN
    dma = pltpu.SemaphoreType.DMA
    steps = zl + half + 1
    vmem = pl.BlockSpec(memory_space=pltpu.VMEM)
    total = dp * experts * (MAIN + TAIL)
    return pl.pallas_call(
        functools.partial(kernel, (dp, yc, zl, width)),
        out_shape=jax.ShapeDtypeStruct((1, total, hidden), jnp.bfloat16),
        in_specs=[vmem, vmem, vmem, pl.BlockSpec(memory_space=pl.ANY)],
        out_specs=vmem,
        scratch_shapes=[
            pltpu.VMEM((experts, *chunk), jnp.bfloat16),
            pltpu.VMEM((ring, dp, yc, *chunk), jnp.bfloat16),
            pltpu.VMEM((zl, yc, *chunk), jnp.bfloat16),
            pltpu.VMEM(down_weight.shape[1:], jnp.bfloat16),
            pltpu.VMEM((2, count, hidden), jnp.float32),
            pltpu.VMEM((2, count, hidden), jnp.float32),
            dma,
            dma((2, yc)), dma((2, yc)),
            dma((2, steps)), dma((2, steps)),
            dma((2, half + 1)), dma((2, half + 1)),
            dma((2, ring)), dma((2, ring)),
            dma((2, ring)), dma((2, ring)),
        ],
        compiler_params=pltpu.CompilerParams(
            collective_id=0, has_side_effects=True, vmem_limit_bytes=48 * 1024 * 1024
        ),
        cost_estimate=pl.CostEstimate(
            flops=2 * total * hidden * width * zl,
            bytes_accessed=2 * (down_weight.size + total * hidden),
            transcendentals=0,
        ),
    )(layer_grad, gate_probs.T, expert_ids.T, down_weight)


def solution(mesh):
    placed = (
        P(("dp", "expert"), "tensor"),
        P(("dp", "expert"), None),
        P(("dp", "expert"), None),
        P("expert", ("dp", "tensor"), None),
    )
    return jax.shard_map(
        body,
        mesh=mesh,
        in_specs=placed,
        out_specs=P("expert", None, ("dp", "tensor")),
        check_vma=False,
    )
```

```python
import functools

import jax
import jax.numpy as jnp
from jax import lax
from jax.experimental import pallas as pl
from jax.experimental.pallas import tpu as pltpu
from jax.sharding import PartitionSpec as P

MESH = pl.DeviceIdType.MESH
MAIN = 16
TAIL = 4


def kernel(
    shape,
    feats_in, probs_in, ids_in, weight, out,
    feats, probs, ids, in_sem, routed, rows, passing, weights, acc, sums_out, sums_in, w_sem,
    a_send, a_recv, z_send, z_recv, t_send, t_recv, x_send, x_recv, v_send, v_recv, s_send, s_recv,
):
    dp, yc, zl, width = shape
    half = zl // 2
    ring = 2 * zl
    quarter = width // 4
    experts = 2 * yc
    x = lax.axis_index("dp")
    ex = lax.axis_index("expert")
    j = lax.axis_index("tensor")
    zh, c = ex // yc, ex % yc
    p = zh * zl + j

    def at_ring(pos):
        pos = (pos + ring) % ring
        return {"expert": (pos // zl) * yc + c, "tensor": pos % zl}

    def at_x(offset):
        return {"dp": (x + offset + dp) % dp}

    def at_c(offset):
        return {"expert": zh * yc + (c + offset) % yc}

    loads = [
        pltpu.make_async_copy(source, target, in_sem.at[i])
        for i, (source, target) in enumerate([(ids_in, ids), (probs_in, probs), (feats_in, feats)])
    ]
    for load in loads:
        load.start()
    barrier = pltpu.get_barrier_semaphore()
    partners = [at_ring(p + 1), at_ring(p - 1), at_x(1), at_x(-1)] + [at_c(i) for i in range(1, yc)]
    for partner in partners:
        pl.semaphore_signal(barrier, inc=1, device_id=partner, device_id_type=MESH)

    hidden = weight.shape[1]
    w_copies = [
        pltpu.make_async_copy(
            weight.at[0, :, pl.ds(s * width, width)], weights.at[s, pl.ds(0, hidden)], w_sem.at[s]
        )
        for s in range(zl)
    ]
    for w_copy in w_copies:
        w_copy.start()

    for load in loads:
        load.wait()
    tokens = feats.shape[0]
    who = [ids[k : k + 1, :] for k in range(2)]
    e_iota = lax.broadcasted_iota(jnp.int32, (experts, tokens), 0)
    named = [(e_iota == who[k]).astype(jnp.float32) for k in range(2)]
    before = lax.broadcasted_iota(jnp.int32, (tokens, tokens), 0) < lax.broadcasted_iota(jnp.int32, (tokens, tokens), 1)
    earlier = jnp.dot(
        (named[0] + named[1]).astype(jnp.bfloat16),
        jnp.where(before, 1.0, 0.0).astype(jnp.bfloat16),
        preferred_element_type=jnp.float32,
    )
    ranks = [
        jnp.sum(earlier * named[0], axis=0, keepdims=True).astype(jnp.int32),
        jnp.sum((earlier + named[0]) * named[1], axis=0, keepdims=True).astype(jnp.int32),
    ]
    row = lax.broadcasted_iota(jnp.int32, (experts * MAIN, tokens), 0)
    sub = lax.broadcasted_iota(jnp.int32, (experts * MAIN, quarter), 0) % MAIN // TAIL

    def gather(codes, wanted):
        hits = [codes[k] == wanted for k in range(2)]
        pick = jnp.where(hits[0] | hits[1], 1.0, 0.0).astype(jnp.bfloat16)
        scale = jnp.where(hits[0], probs[0:1, :], 0.0) + jnp.where(hits[1], probs[1:2, :], 0.0)
        scale = jnp.sum(scale, axis=1, keepdims=True)
        return jnp.dot(pick, feats[...], preferred_element_type=jnp.float32), scale

    got, scale = gather([jnp.where(ranks[k] < MAIN, who[k] * MAIN + ranks[k], -1) for k in range(2)], row)
    routed[:, :, 0:width] = (got * scale).astype(jnp.bfloat16).reshape(experts, MAIN, width)
    got, scale = gather(
        [jnp.where(ranks[k] >= MAIN, who[k] * TAIL + ranks[k] - MAIN, -1) for k in range(2)],
        row // MAIN * TAIL + row % TAIL,
    )
    tail = jnp.zeros((experts * MAIN, quarter), jnp.float32)
    for q in range(4):
        tail = tail + jnp.where(sub == q, got[:, q * quarter : (q + 1) * quarter], 0.0)
    routed[:, :, width : width + quarter] = (tail * scale).astype(jnp.bfloat16).reshape(experts, MAIN, quarter)

    pl.semaphore_wait(barrier, len(partners))

    def beside(parity):
        return jnp.where((x + parity) % 2 == 0, -1, 1)

    def v_copy(s):
        return pltpu.make_async_remote_copy(
            src_ref=weights.at[s, pl.ds(0, hidden)],
            dst_ref=weights.at[s, pl.ds(hidden, hidden)],
            send_sem=v_send.at[s],
            recv_sem=v_recv.at[s],
            device_id=at_x(beside(1 - s % 2)),
            device_id_type=MESH,
        )

    for s in range(zl):
        w_copies[s].wait()
        v_copy(s).start()

    def a_copy(i, other):
        target = (c + i) % yc
        source = routed.at[((1 - zh) if other else zh) * yc + target]
        return pltpu.make_async_remote_copy(
            src_ref=source,
            dst_ref=passing.at[j, c] if other else rows.at[p, 0, c],
            send_sem=a_send.at[other, i],
            recv_sem=a_recv.at[other, i],
            device_id=at_c(i),
            device_id_type=MESH,
        )

    def a_arrived(i, other):
        origin = (c + yc - i) % yc
        place = passing.at[j, origin] if other else rows.at[p, 0, origin]
        pltpu.make_async_copy(place, place, a_recv.at[other, i]).wait()

    piece = yc // 2

    def unit_of(way, step):
        return (p + (step if way else -step) + ring) % ring

    def along(way):
        return zl - 1 - j if way else j

    def z_place(way, step, h):
        return rows.at[unit_of(way, step), 0, pl.ds(h * piece, piece)]

    def t_place(way, step, h):
        return passing.at[(j + (step if way else -step) + zl) % zl, pl.ds(h * piece, piece)]

    def z_copy(way, step, h):
        return pltpu.make_async_remote_copy(
            src_ref=z_place(way, step, h),
            dst_ref=z_place(way, step, h),
            send_sem=z_send.at[way, step, h],
            recv_sem=z_recv.at[way, step + 1, h],
            device_id=at_ring(p + (-1 if way else 1)),
            device_id_type=MESH,
        )

    def t_copy(way, step, h, leaves):
        return pltpu.make_async_remote_copy(
            src_ref=t_place(way, step, h),
            dst_ref=(z_place if leaves else t_place)(way, step, h),
            send_sem=t_send.at[way, step, h],
            recv_sem=(z_recv if leaves else t_recv).at[way, step + 1, h],
            device_id=at_ring(p + (-1 if way else 1)),
            device_id_type=MESH,
        )

    def z_start(way, step, h):
        @pl.when((along(way) < zl - 1) & (step <= along(way) + half))
        def _():
            z_copy(way, step, h).start()

    def t_start(way, step, h):
        q = along(way)

        @pl.when((q < zl - 1) & (step <= q - half))
        def _():
            t_copy(way, step, h, False).start()

        @pl.when((q == zl - 1) & (step <= q - half))
        def _():
            t_copy(way, step, h, True).start()

    def x_copy(unit):
        return pltpu.make_async_remote_copy(
            src_ref=rows.at[unit, 0],
            dst_ref=rows.at[unit, 1],
            send_sem=x_send.at[unit],
            recv_sem=x_recv.at[unit],
            device_id=at_x(beside(unit % 2)),
            device_id_type=MESH,
        )

    def z_round(step):
        for h in range(2):
            for way in range(2):
                @pl.when(step <= along(way) + half)
                def _():
                    place = z_place(way, step, h)
                    pltpu.make_async_copy(place, place, z_recv.at[way, step, h]).wait()

                z_start(way, step, h)

                @pl.when(step <= along(way) - half)
                def _():
                    place = t_place(way, step, h)
                    pltpu.make_async_copy(place, place, t_recv.at[way, step, h]).wait()

                t_start(way, step, h)
        for way in range(2):
            @pl.when(step <= along(way) + half)
            def _():
                x_copy(unit_of(way, step)).start()

    up, down = j + half, zl - 1 - j + half
    both = jnp.minimum(up, down)

    def unit_at(m):
        paired = m <= 2 * both
        step = jnp.where(paired, (m + 1) // 2, m - both)
        goes_up = jnp.where(paired, m % 2 == 1, up > down)
        return (p + jnp.where(goes_up, -step, step) + ring) % ring

    count = yc * MAIN

    def work(unit):
        place = rows.at[unit, 1]
        pltpu.make_async_copy(place, place, x_recv.at[unit]).wait()
        zone, s = unit // zl, unit % zl
        w = weights[s]
        contract = (((1,), (1,)), ((), ()))
        whole = rows[unit, :, :, :, 0:width].reshape(2 * count, width)
        acc[s % 2, zone, 0] += lax.dot_general(whole, w, contract, preferred_element_type=jnp.float32)
        quarters = rows[unit, :, :, :, width : width + quarter].reshape(2 * count, quarter)
        of = lax.broadcasted_iota(jnp.int32, (2 * count, quarter), 0) % MAIN // TAIL
        spread = jnp.concatenate(
            [jnp.where(of == q, quarters, jnp.zeros_like(quarters)) for q in range(4)], axis=1
        )
        acc[s % 2, zone, 1] += lax.dot_general(spread, w, contract, preferred_element_type=jnp.float32)

    slots = MAIN + TAIL
    out_row = lax.broadcasted_iota(jnp.int32, (yc * slots, yc * (MAIN + 8)), 0)
    in_row = lax.broadcasted_iota(jnp.int32, (yc * slots, yc * (MAIN + 8)), 1)
    group, slot = out_row // slots, out_row % slots
    source = jnp.where(slot < MAIN, group * MAIN + slot, count + group * 8 + slot - MAIN)
    order = jnp.where(source == in_row, 1.0, 0.0).astype(jnp.bfloat16)

    def in_order(main, ends):
        ends = ends.reshape(yc, MAIN, ends.shape[-1])
        ends = (ends[:, 0:8, :] + ends[:, 8:16, :]).reshape(yc * 8, ends.shape[-1])
        ends = ends + pltpu.roll(ends, yc * 8 - TAIL, 0)
        both_parts = jnp.concatenate([main.astype(jnp.bfloat16), ends.astype(jnp.bfloat16)], axis=0)
        return jnp.dot(order, both_parts, preferred_element_type=jnp.float32)

    def s_copy(parity, zone):
        return pltpu.make_async_remote_copy(
            src_ref=sums_out.at[parity, zone],
            dst_ref=sums_in.at[parity, zone],
            send_sem=s_send.at[parity, zone],
            recv_sem=s_recv.at[parity, zone],
            device_id=at_x(beside(1 - parity)),
            device_id_type=MESH,
        )

    def give(zone):
        for parity in range(2):
            for col in range(2):
                at = pl.ds(col * count, count)
                theirs = pl.ds(hidden, hidden)
                part = in_order(acc[parity, zone, 0, at, theirs], acc[parity, zone, 1, at, theirs])
                sums_out[parity, zone, col] = part.astype(jnp.bfloat16)
            s_copy(parity, zone).start()

    def store(column, zone, value):
        start = pl.multiple_of((column * 2 + zone) * yc * slots, MAIN)
        out[0, pl.ds(start, yc * slots), :] = value.astype(jnp.bfloat16)

    def finish(zone):
        mine = pl.ds(0, hidden)
        own, next_to = pl.ds(0, count), pl.ds(count, count)
        store(x, zone, in_order(
            acc[0, zone, 0, own, mine] + acc[1, zone, 0, own, mine],
            acc[0, zone, 1, own, mine] + acc[1, zone, 1, own, mine],
        ))
        local = [in_order(acc[k, zone, 0, next_to, mine], acc[k, zone, 1, next_to, mine]) for k in range(2)]
        for parity in range(2):
            place = sums_in.at[parity, zone]
            pltpu.make_async_copy(place, place, s_recv.at[parity, zone]).wait()
        for parity in range(2):
            column = (x + beside(parity) + dp) % dp
            store(column, zone, local[parity] + sums_in[1 - parity, zone, 0].astype(jnp.float32))
        store((x + 2) % dp, zone, sums_in[0, zone, 1].astype(jnp.float32) + sums_in[1, zone, 1].astype(jnp.float32))

    for other in range(2):
        for i in range(1, yc):
            a_copy(i, other).start()
    rows[p, 0, c] = routed[zh * yc + c]
    passing[j, c] = routed[(1 - zh) * yc + c]
    acc[...] = jnp.zeros_like(acc)
    for i in range(1, yc):
        a_arrived(i, 0)
    for h in range(2):
        for way in range(2):
            z_start(way, 0, h)
    x_copy(p).start()
    for i in range(1, yc):
        a_arrived(i, 1)
    for h in range(2):
        for way in range(2):
            t_start(way, 0, h)

    late = half + 1

    def turn(r, carry):
        z_round(r + 1)

        @pl.when(r == late)
        def _():
            for s in range(zl):
                place = weights.at[s, pl.ds(hidden, hidden)]
                pltpu.make_async_copy(place, place, v_recv.at[s]).wait()

        @pl.when(r >= late)
        def _():
            work(unit_at(2 * (r - late)))
            work(unit_at(2 * (r - late) + 1))

        @pl.when(r == late + (zl - 1 + half) // 2)
        def _():
            give(zh)

        return carry

    lax.fori_loop(0, late + zl, turn, 0)
    give(1 - zh)
    finish(zh)
    finish(1 - zh)

    for other in range(2):
        for i in range(1, yc):
            a_copy(i, other).wait_send()
    for s in range(zl):
        v_copy(s).wait_send()
    for parity in range(2):
        for zone in range(2):
            s_copy(parity, zone).wait_send()

    def left(step, carry):
        for way in range(2):
            q = along(way)
            for h in range(2):
                @pl.when((q < zl - 1) & (step <= q + half))
                def _():
                    z_copy(way, step, h).wait_send()

                @pl.when(step <= q - half)
                def _():
                    t_copy(way, step, h, False).wait_send()

        x_copy(step).wait_send()
        return carry

    lax.fori_loop(0, ring, left, 0)


def body(layer_grad, gate_probs, expert_ids, down_weight):
    dp, zl = lax.axis_size("dp"), lax.axis_size("tensor")
    experts = down_weight.shape[0] * lax.axis_size("expert")
    yc = experts // 2
    ring = 2 * zl
    width = layer_grad.shape[1]
    hidden = down_weight.shape[1]
    half = zl // 2
    chunk = (MAIN, width + width // 4)
    dma = pltpu.SemaphoreType.DMA
    steps = zl + half + 1
    vmem = pl.BlockSpec(memory_space=pltpu.VMEM)
    total = dp * experts * (MAIN + TAIL)
    return pl.pallas_call(
        functools.partial(kernel, (dp, yc, zl, width)),
        out_shape=jax.ShapeDtypeStruct((1, total, hidden), jnp.bfloat16),
        in_specs=[pl.BlockSpec(memory_space=pl.ANY)] * 4,
        out_specs=vmem,
        scratch_shapes=[
            pltpu.VMEM(layer_grad.shape, jnp.bfloat16),
            pltpu.VMEM((2, layer_grad.shape[0]), jnp.float32),
            pltpu.VMEM((2, layer_grad.shape[0]), jnp.int32),
            dma((3,)),
            pltpu.VMEM((experts, *chunk), jnp.bfloat16),
            pltpu.VMEM((ring, 2, yc, *chunk), jnp.bfloat16),
            pltpu.VMEM((zl, yc, *chunk), jnp.bfloat16),
            pltpu.VMEM((zl, 2 * hidden, width), jnp.bfloat16),
            pltpu.VMEM((2, 2, 2, 2 * yc * MAIN, 2 * hidden), jnp.float32),
            pltpu.VMEM((2, 2, 2, yc * (MAIN + TAIL), hidden), jnp.bfloat16),
            pltpu.VMEM((2, 2, 2, yc * (MAIN + TAIL), hidden), jnp.bfloat16),
            dma((zl,)),
            dma((2, yc)), dma((2, yc)),
            dma((2, steps, 2)), dma((2, steps, 2)),
            dma((2, half + 1, 2)), dma((2, half + 1, 2)),
            dma((ring,)), dma((ring,)),
            dma((zl,)), dma((zl,)),
            dma((2, 2)), dma((2, 2)),
        ],
        compiler_params=pltpu.CompilerParams(
            collective_id=0, has_side_effects=True, vmem_limit_bytes=62 * 1024 * 1024
        ),
        cost_estimate=pl.CostEstimate(
            flops=2 * total * hidden * width * zl,
            bytes_accessed=2 * (down_weight.size + total * hidden),
            transcendentals=0,
        ),
    )(layer_grad, gate_probs.T, expert_ids.T, down_weight)


def solution(mesh):
    placed = (
        P(("dp", "expert"), "tensor"),
        P(("dp", "expert"), None),
        P(("dp", "expert"), None),
        P("expert", ("dp", "tensor"), None),
    )
    return jax.shard_map(
        body,
        mesh=mesh,
        in_specs=placed,
        out_specs=P("expert", None, ("dp", "tensor")),
        check_vma=False,
    )
```

```python
import functools

import jax
import jax.numpy as jnp
from jax import lax
from jax.experimental import pallas as pl
from jax.experimental.pallas import tpu as pltpu
from jax.sharding import PartitionSpec as P

MESH = pl.DeviceIdType.MESH
MAIN = 16
TAIL = 4


def kernel(
    shape,
    feats_in, probs_in, ids_in, weight, out,
    feats, probs, ids, in_sem, routed, rows, passing, weights, acc, sums_out, sums_in, w_sem,
    a_send, a_recv, z_send, z_recv, t_send, t_recv, x_send, x_recv, v_send, v_recv, s_send, s_recv,
):
    dp, yc, zl, width = shape
    half = zl // 2
    ring = 2 * zl
    quarter = width // 4
    experts = 2 * yc
    x = lax.axis_index("dp")
    ex = lax.axis_index("expert")
    j = lax.axis_index("tensor")
    zh, c = ex // yc, ex % yc
    p = zh * zl + j

    def at_ring(pos):
        pos = (pos + ring) % ring
        return {"expert": (pos // zl) * yc + c, "tensor": pos % zl}

    def at_x(offset):
        return {"dp": (x + offset + dp) % dp}

    def at_c(offset):
        return {"expert": zh * yc + (c + offset) % yc}

    loads = [
        pltpu.make_async_copy(source, target, in_sem.at[i])
        for i, (source, target) in enumerate([(ids_in, ids), (probs_in, probs), (feats_in, feats)])
    ]
    for load in loads:
        load.start()
    short, long = jnp.minimum(j, zl - 1 - j), jnp.maximum(j, zl - 1 - j)
    long_up = j > zl - 1 - j

    def unit_at(m):
        paired = m <= 2 * short
        native = m < zl
        step = jnp.where(paired, (m + 1) // 2, m - short)
        goes_up = jnp.where(paired, m % 2 == 1, long_up)
        far = m - zl
        step = jnp.where(native, step, jnp.where(far < half, short + 1 + far, long + 1 + far - half))
        goes_up = jnp.where(native, goes_up, jnp.where(far < half, ~long_up, long_up))
        return (p + jnp.where(goes_up, -step, step) + ring) % ring

    barrier = pltpu.get_barrier_semaphore()
    partners = [at_ring(p + 1), at_ring(p - 1), at_x(1), at_x(-1)] + [at_c(i) for i in range(1, yc)]
    for partner in partners:
        pl.semaphore_signal(barrier, inc=1, device_id=partner, device_id_type=MESH)

    hidden = weight.shape[1]
    w_copies = [
        pltpu.make_async_copy(
            weight.at[0, :, pl.ds(s * width, width)], weights.at[s, pl.ds(0, hidden)], w_sem.at[s]
        )
        for s in range(zl)
    ]
    for w_copy in w_copies:
        w_copy.start()

    for load in loads:
        load.wait()
    tokens = feats.shape[0]
    who = [ids[k : k + 1, :] for k in range(2)]
    e_iota = lax.broadcasted_iota(jnp.int32, (experts, tokens), 0)
    named = [(e_iota == who[k]).astype(jnp.float32) for k in range(2)]
    before = lax.broadcasted_iota(jnp.int32, (tokens, tokens), 0) < lax.broadcasted_iota(jnp.int32, (tokens, tokens), 1)
    earlier = jnp.dot(
        (named[0] + named[1]).astype(jnp.bfloat16),
        jnp.where(before, 1.0, 0.0).astype(jnp.bfloat16),
        preferred_element_type=jnp.float32,
    )
    ranks = [
        jnp.sum(earlier * named[0], axis=0, keepdims=True).astype(jnp.int32),
        jnp.sum((earlier + named[0]) * named[1], axis=0, keepdims=True).astype(jnp.int32),
    ]
    row = lax.broadcasted_iota(jnp.int32, (experts * MAIN, tokens), 0)
    sub = lax.broadcasted_iota(jnp.int32, (experts * MAIN, quarter), 0) % MAIN // TAIL

    def gather(codes, wanted):
        hits = [codes[k] == wanted for k in range(2)]
        pick = jnp.where(hits[0] | hits[1], 1.0, 0.0).astype(jnp.bfloat16)
        scale = jnp.where(hits[0], probs[0:1, :], 0.0) + jnp.where(hits[1], probs[1:2, :], 0.0)
        scale = jnp.sum(scale, axis=1, keepdims=True)
        return jnp.dot(pick, feats[...], preferred_element_type=jnp.float32), scale

    got, scale = gather([jnp.where(ranks[k] < MAIN, who[k] * MAIN + ranks[k], -1) for k in range(2)], row)
    routed[:, :, 0:width] = (got * scale).astype(jnp.bfloat16).reshape(experts, MAIN, width)
    pl.semaphore_wait(barrier, len(partners))

    beside = jnp.where((x + c) % 2 == 0, -1, 1)

    def v_copy(s):
        return pltpu.make_async_remote_copy(
            src_ref=weights.at[s, pl.ds(0, hidden)],
            dst_ref=weights.at[s, pl.ds(hidden, hidden)],
            send_sem=v_send.at[s],
            recv_sem=v_recv.at[s],
            device_id=at_x(-beside),
            device_id_type=MESH,
        )

    for s in range(zl):
        w_copies[s].wait()
    for m in range(zl):
        v_copy(unit_at(m) % zl).start()

    got, scale = gather(
        [jnp.where(ranks[k] >= MAIN, who[k] * TAIL + ranks[k] - MAIN, -1) for k in range(2)],
        row // MAIN * TAIL + row % TAIL,
    )
    tail = jnp.zeros((experts * MAIN, quarter), jnp.float32)
    for q in range(4):
        tail = tail + jnp.where(sub == q, got[:, q * quarter : (q + 1) * quarter], 0.0)
    routed[:, :, width : width + quarter] = (tail * scale).astype(jnp.bfloat16).reshape(experts, MAIN, quarter)

    def a_copy(i, other):
        target = (c + i) % yc
        source = routed.at[((1 - zh) if other else zh) * yc + target]
        return pltpu.make_async_remote_copy(
            src_ref=source,
            dst_ref=passing.at[j, c] if other else rows.at[p, 0, c],
            send_sem=a_send.at[other, i],
            recv_sem=a_recv.at[other, i],
            device_id=at_c(i),
            device_id_type=MESH,
        )

    def a_arrived(i, other):
        origin = (c + yc - i) % yc
        place = passing.at[j, origin] if other else rows.at[p, 0, origin]
        pltpu.make_async_copy(place, place, a_recv.at[other, i]).wait()

    piece = yc // 2

    def unit_of(way, step):
        return (p + (step if way else -step) + ring) % ring

    def along(way):
        return zl - 1 - j if way else j

    def z_place(way, step, h):
        return rows.at[unit_of(way, step), 0, pl.ds(h * piece, piece)]

    def t_place(way, step, h):
        return passing.at[(j + (step if way else -step) + zl) % zl, pl.ds(h * piece, piece)]

    def z_copy(way, step, h):
        return pltpu.make_async_remote_copy(
            src_ref=z_place(way, step, h),
            dst_ref=z_place(way, step, h),
            send_sem=z_send.at[way, step, h],
            recv_sem=z_recv.at[way, step + 1, h],
            device_id=at_ring(p + (-1 if way else 1)),
            device_id_type=MESH,
        )

    def t_copy(way, step, h, leaves):
        return pltpu.make_async_remote_copy(
            src_ref=t_place(way, step, h),
            dst_ref=(z_place if leaves else t_place)(way, step, h),
            send_sem=t_send.at[way, step, h],
            recv_sem=(z_recv if leaves else t_recv).at[way, step + 1, h],
            device_id=at_ring(p + (-1 if way else 1)),
            device_id_type=MESH,
        )

    def z_start(way, step, h):
        @pl.when((along(way) < zl - 1) & (step <= along(way) + half))
        def _():
            z_copy(way, step, h).start()

    def t_start(way, step, h):
        q = along(way)

        @pl.when((q < zl - 1) & (step <= q - half))
        def _():
            t_copy(way, step, h, False).start()

        @pl.when((q == zl - 1) & (step <= q - half))
        def _():
            t_copy(way, step, h, True).start()

    def x_copy(unit, h):
        return pltpu.make_async_remote_copy(
            src_ref=rows.at[unit, 0, pl.ds(h * piece, piece)],
            dst_ref=rows.at[unit, 1, pl.ds(h * piece, piece)],
            send_sem=x_send.at[unit, h],
            recv_sem=x_recv.at[unit, h],
            device_id=at_x(beside),
            device_id_type=MESH,
        )

    def z_round(step):
        for h in range(2):
            for way in range(2):
                @pl.when(step <= along(way) + half)
                def _():
                    place = z_place(way, step, h)
                    pltpu.make_async_copy(place, place, z_recv.at[way, step, h]).wait()

                z_start(way, step, h)

                @pl.when(step <= along(way) + half)
                def _():
                    x_copy(unit_of(way, step), h).start()

                @pl.when(step <= along(way) - half)
                def _():
                    place = t_place(way, step, h)
                    pltpu.make_async_copy(place, place, t_recv.at[way, step, h]).wait()

                t_start(way, step, h)

    count = yc * MAIN

    def work(m):
        unit = unit_at(m)
        for h in range(2):
            place = rows.at[unit, 1, pl.ds(h * piece, piece)]
            pltpu.make_async_copy(place, place, x_recv.at[unit, h]).wait()
        zone, s = unit // zl, unit % zl

        @pl.when(m < zl)
        def _():
            theirs = weights.at[s, pl.ds(hidden, hidden)]
            pltpu.make_async_copy(theirs, theirs, v_recv.at[s]).wait()

        w = weights[s]
        contract = (((1,), (1,)), ((), ()))
        whole = rows[unit, :, :, :, 0:width].reshape(2 * count, width)
        acc[zone, 0] += lax.dot_general(whole, w, contract, preferred_element_type=jnp.float32)
        quarters = rows[unit, :, :, :, width : width + quarter].reshape(2 * count, quarter)
        of = lax.broadcasted_iota(jnp.int32, (2 * count, quarter), 0) % MAIN // TAIL
        spread = jnp.concatenate(
            [jnp.where(of == q, quarters, jnp.zeros_like(quarters)) for q in range(4)], axis=1
        )
        acc[zone, 1] += lax.dot_general(spread, w, contract, preferred_element_type=jnp.float32)

    slots = MAIN + TAIL
    out_row = lax.broadcasted_iota(jnp.int32, (yc * slots, yc * (MAIN + 8)), 0)
    in_row = lax.broadcasted_iota(jnp.int32, (yc * slots, yc * (MAIN + 8)), 1)
    group, slot = out_row // slots, out_row % slots
    source = jnp.where(slot < MAIN, group * MAIN + slot, count + group * 8 + slot - MAIN)
    order = jnp.where(source == in_row, 1.0, 0.0).astype(jnp.bfloat16)

    def in_order(main, ends):
        ends = ends.reshape(yc, MAIN, ends.shape[-1])
        ends = (ends[:, 0:8, :] + ends[:, 8:16, :]).reshape(yc * 8, ends.shape[-1])
        ends = ends + pltpu.roll(ends, yc * 8 - TAIL, 0)
        both_parts = jnp.concatenate([main.astype(jnp.bfloat16), ends.astype(jnp.bfloat16)], axis=0)
        return jnp.dot(order, both_parts, preferred_element_type=jnp.float32)

    def s_copy(zone, col):
        return pltpu.make_async_remote_copy(
            src_ref=sums_out.at[zone, col],
            dst_ref=sums_in.at[zone, col],
            send_sem=s_send.at[zone, col],
            recv_sem=s_recv.at[zone, col],
            device_id=at_x(-beside),
            device_id_type=MESH,
        )

    def part(zone, col, cols):
        at = pl.ds(col * count, count)
        return in_order(acc[zone, 0, at, cols], acc[zone, 1, at, cols]).astype(jnp.bfloat16)

    def give(zone):
        for col in range(2):
            sums_out[zone, col] = part(zone, col, pl.ds(hidden, hidden))
            s_copy(zone, col).start()

    def store(column, zone, value):
        start = pl.multiple_of(((column + dp) % dp * 2 + zone) * yc * slots, MAIN)
        out[0, pl.ds(start, yc * slots), :] = value

    def keep(zone):
        for col in range(2):
            store(x + col * beside, zone, part(zone, col, pl.ds(0, hidden)))

    def take(zone):
        for col in range(2):
            place = sums_in.at[zone, col]
            pltpu.make_async_copy(place, place, s_recv.at[zone, col]).wait()
            store(x + (2 if col else -beside), zone, sums_in[zone, col])

    for other in range(2):
        for i in range(1, yc):
            a_copy(i, other).start()
    rows[p, 0, c] = routed[zh * yc + c]
    passing[j, c] = routed[(1 - zh) * yc + c]
    acc[...] = jnp.zeros_like(acc)
    for i in range(1, yc):
        a_arrived(i, 0)
    for h in range(2):
        for way in range(2):
            z_start(way, 0, h)
    for h in range(2):
        x_copy(p, h).start()
    for i in range(1, yc):
        a_arrived(i, 1)
    for h in range(2):
        for way in range(2):
            t_start(way, 0, h)

    late = half + 2

    def turn(r, carry):
        z_round(r + 1)


        @pl.when(r >= late)
        def _():
            work(2 * (r - late))
            work(2 * (r - late) + 1)

        @pl.when(r == late + zl // 2 - 1)
        def _():
            give(zh)

        return carry

    lax.fori_loop(0, late + zl, turn, 0)
    give(1 - zh)
    keep(zh)
    take(zh)
    keep(1 - zh)
    take(1 - zh)

    for other in range(2):
        for i in range(1, yc):
            a_copy(i, other).wait_send()
    for s in range(zl):
        v_copy(s).wait_send()
    for zone in range(2):
        for col in range(2):
            s_copy(zone, col).wait_send()

    def left(step, carry):
        for way in range(2):
            q = along(way)
            for h in range(2):
                @pl.when((q < zl - 1) & (step <= q + half))
                def _():
                    z_copy(way, step, h).wait_send()

                @pl.when(step <= q - half)
                def _():
                    t_copy(way, step, h, False).wait_send()

        for h in range(2):
            x_copy(step, h).wait_send()
        return carry

    lax.fori_loop(0, ring, left, 0)


def body(layer_grad, gate_probs, expert_ids, down_weight):
    dp, zl = lax.axis_size("dp"), lax.axis_size("tensor")
    experts = down_weight.shape[0] * lax.axis_size("expert")
    yc = experts // 2
    ring = 2 * zl
    width = layer_grad.shape[1]
    hidden = down_weight.shape[1]
    half = zl // 2
    chunk = (MAIN, width + width // 4)
    dma = pltpu.SemaphoreType.DMA
    steps = zl + half + 1
    vmem = pl.BlockSpec(memory_space=pltpu.VMEM)
    total = dp * experts * (MAIN + TAIL)
    return pl.pallas_call(
        functools.partial(kernel, (dp, yc, zl, width)),
        out_shape=pltpu.VMEM((1, total, hidden), jnp.bfloat16),
        in_specs=[pl.BlockSpec(memory_space=pltpu.HBM)] * 4,
        out_specs=vmem,
        scratch_shapes=[
            pltpu.VMEM(layer_grad.shape, jnp.bfloat16),
            pltpu.VMEM((2, layer_grad.shape[0]), jnp.float32),
            pltpu.VMEM((2, layer_grad.shape[0]), jnp.int32),
            dma((3,)),
            pltpu.VMEM((experts, *chunk), jnp.bfloat16),
            pltpu.VMEM((ring, 2, yc, *chunk), jnp.bfloat16),
            pltpu.VMEM((zl, yc, *chunk), jnp.bfloat16),
            pltpu.VMEM((zl, 2 * hidden, width), jnp.bfloat16),
            pltpu.VMEM((2, 2, 2 * yc * MAIN, 2 * hidden), jnp.float32),
            pltpu.VMEM((2, 2, yc * (MAIN + TAIL), hidden), jnp.bfloat16),
            pltpu.VMEM((2, 2, yc * (MAIN + TAIL), hidden), jnp.bfloat16),
            dma((zl,)),
            dma((2, yc)), dma((2, yc)),
            dma((2, steps, 2)), dma((2, steps, 2)),
            dma((2, half + 1, 2)), dma((2, half + 1, 2)),
            dma((ring, 2)), dma((ring, 2)),
            dma((zl,)), dma((zl,)),
            dma((2, 2)), dma((2, 2)),
        ],
        compiler_params=pltpu.CompilerParams(
            collective_id=0, has_side_effects=True, vmem_limit_bytes=56 * 1024 * 1024
        ),
        cost_estimate=pl.CostEstimate(
            flops=2 * total * hidden * width * zl,
            bytes_accessed=2 * (down_weight.size + total * hidden),
            transcendentals=0,
        ),
    )(layer_grad, gate_probs.T, expert_ids.T, down_weight)


def solution(mesh):
    placed = (
        P(("dp", "expert"), "tensor"),
        P(("dp", "expert"), None),
        P(("dp", "expert"), None),
        P("expert", ("dp", "tensor"), None),
    )
    return jax.shard_map(
        body,
        mesh=mesh,
        in_specs=placed,
        out_specs=P("expert", None, ("dp", "tensor")),
        check_vma=False,
    )
```

```python
import functools

import jax
import jax.numpy as jnp
from jax import lax
from jax.experimental import pallas as pl
from jax.experimental.pallas import tpu as pltpu
from jax.sharding import PartitionSpec as P

MESH = pl.DeviceIdType.MESH
MAIN = 16
TAIL = 4


def kernel(
    shape,
    feats_in, probs_in, ids_in, weight, out,
    feats, probs, ids, in_sem, routed, rows, passing, weights, acc, sums_out, sums_in, w_sem,
    a_send, a_recv, z_send, z_recv, t_send, t_recv, x_send, x_recv, v_send, v_recv, s_send, s_recv, e_send, e_recv,
):
    dp, yc, zl, width = shape
    half = zl // 2
    ring = 2 * zl
    quarter = width // 4
    experts = 2 * yc
    x = lax.axis_index("dp")
    ex = lax.axis_index("expert")
    j = lax.axis_index("tensor")
    zh, c = ex // yc, ex % yc
    p = zh * zl + j

    def at_ring(pos):
        pos = (pos + ring) % ring
        return {"expert": (pos // zl) * yc + c, "tensor": pos % zl}

    def at_x(offset):
        return {"dp": (x + offset + dp) % dp}

    def at_c(offset):
        return {"expert": zh * yc + (c + offset) % yc}

    loads = [
        pltpu.make_async_copy(source, target, in_sem.at[i])
        for i, (source, target) in enumerate([(ids_in, ids), (probs_in, probs), (feats_in, feats)])
    ]
    for load in loads:
        load.start()
    short, long = jnp.minimum(j, zl - 1 - j), jnp.maximum(j, zl - 1 - j)
    long_up = j > zl - 1 - j

    def unit_at(m):
        paired = m <= 2 * short
        native = m < zl
        step = jnp.where(paired, (m + 1) // 2, m - short)
        goes_up = jnp.where(paired, m % 2 == 1, long_up)
        far = m - zl
        step = jnp.where(native, step, jnp.where(far < half, short + 1 + far, long + 1 + far - half))
        goes_up = jnp.where(native, goes_up, jnp.where(far < half, ~long_up, long_up))
        return (p + jnp.where(goes_up, -step, step) + ring) % ring

    barrier = pltpu.get_barrier_semaphore()
    partners = [at_ring(p + 1), at_ring(p - 1), at_x(1), at_x(-1)] + [at_c(i) for i in range(1, yc)]
    for partner in partners:
        pl.semaphore_signal(barrier, inc=1, device_id=partner, device_id_type=MESH)

    hidden = weight.shape[1]
    w_copies = [
        pltpu.make_async_copy(
            weight.at[0, :, pl.ds(s * width, width)], weights.at[s, pl.ds(0, hidden)], w_sem.at[s]
        )
        for s in range(zl)
    ]
    for w_copy in w_copies:
        w_copy.start()

    for load in loads:
        load.wait()
    tokens = feats.shape[0]
    who = [ids[k : k + 1, :] for k in range(2)]
    e_iota = lax.broadcasted_iota(jnp.int32, (experts, tokens), 0)
    named = [(e_iota == who[k]).astype(jnp.float32) for k in range(2)]
    before = lax.broadcasted_iota(jnp.int32, (tokens, tokens), 0) < lax.broadcasted_iota(jnp.int32, (tokens, tokens), 1)
    earlier = jnp.dot(
        (named[0] + named[1]).astype(jnp.bfloat16),
        jnp.where(before, 1.0, 0.0).astype(jnp.bfloat16),
        preferred_element_type=jnp.float32,
    )
    ranks = [
        jnp.sum(earlier * named[0], axis=0, keepdims=True).astype(jnp.int32),
        jnp.sum((earlier + named[0]) * named[1], axis=0, keepdims=True).astype(jnp.int32),
    ]
    row = lax.broadcasted_iota(jnp.int32, (experts * MAIN, tokens), 0)
    sub = lax.broadcasted_iota(jnp.int32, (experts * MAIN, quarter), 0) % MAIN // TAIL

    def gather(codes, wanted):
        hits = [codes[k] == wanted for k in range(2)]
        pick = jnp.where(hits[0] | hits[1], 1.0, 0.0).astype(jnp.bfloat16)
        scale = jnp.where(hits[0], probs[0:1, :], 0.0) + jnp.where(hits[1], probs[1:2, :], 0.0)
        scale = jnp.sum(scale, axis=1, keepdims=True)
        return jnp.dot(pick, feats[...], preferred_element_type=jnp.float32), scale

    got, scale = gather([jnp.where(ranks[k] < MAIN, who[k] * MAIN + ranks[k], -1) for k in range(2)], row)
    routed[:, :, 0:width] = (got * scale).astype(jnp.bfloat16).reshape(experts, MAIN, width)
    pl.semaphore_wait(barrier, len(partners))

    beside = jnp.where((x + c) % 2 == 0, -1, 1)

    def v_copy(s):
        return pltpu.make_async_remote_copy(
            src_ref=weights.at[s, pl.ds(0, hidden)],
            dst_ref=weights.at[s, pl.ds(hidden, hidden)],
            send_sem=v_send.at[s],
            recv_sem=v_recv.at[s],
            device_id=at_x(-beside),
            device_id_type=MESH,
        )

    for s in range(zl):
        w_copies[s].wait()
    for m in range(zl):
        v_copy(unit_at(m) % zl).start()

    got, scale = gather(
        [jnp.where(ranks[k] >= MAIN, who[k] * TAIL + ranks[k] - MAIN, -1) for k in range(2)],
        row // MAIN * TAIL + row % TAIL,
    )
    tail = jnp.zeros((experts * MAIN, quarter), jnp.float32)
    for q in range(4):
        tail = tail + jnp.where(sub == q, got[:, q * quarter : (q + 1) * quarter], 0.0)
    routed[:, :, width : width + quarter] = (tail * scale).astype(jnp.bfloat16).reshape(experts, MAIN, quarter)

    def a_copy(i, other):
        target = (c + i) % yc
        source = routed.at[((1 - zh) if other else zh) * yc + target]
        return pltpu.make_async_remote_copy(
            src_ref=source,
            dst_ref=passing.at[j, c] if other else rows.at[p, 0, c],
            send_sem=a_send.at[other, i],
            recv_sem=a_recv.at[other, i],
            device_id=at_c(i),
            device_id_type=MESH,
        )

    def a_arrived(i, other):
        origin = (c + yc - i) % yc
        place = passing.at[j, origin] if other else rows.at[p, 0, origin]
        pltpu.make_async_copy(place, place, a_recv.at[other, i]).wait()

    piece = yc // 2

    def unit_of(way, step):
        return (p + (step if way else -step) + ring) % ring

    def along(way):
        return zl - 1 - j if way else j

    def z_place(way, step, h):
        return rows.at[unit_of(way, step), 0, pl.ds(h * piece, piece)]

    def t_place(way, step, h):
        return passing.at[(j + (step if way else -step) + zl) % zl, pl.ds(h * piece, piece)]

    def z_copy(way, step, h):
        return pltpu.make_async_remote_copy(
            src_ref=z_place(way, step, h),
            dst_ref=z_place(way, step, h),
            send_sem=z_send.at[way, step, h],
            recv_sem=z_recv.at[way, step + 1, h],
            device_id=at_ring(p + (-1 if way else 1)),
            device_id_type=MESH,
        )

    def t_copy(way, step, h, leaves):
        return pltpu.make_async_remote_copy(
            src_ref=t_place(way, step, h),
            dst_ref=(z_place if leaves else t_place)(way, step, h),
            send_sem=t_send.at[way, step, h],
            recv_sem=(z_recv if leaves else t_recv).at[way, step + 1, h],
            device_id=at_ring(p + (-1 if way else 1)),
            device_id_type=MESH,
        )

    def z_start(way, step, h):
        @pl.when((along(way) < zl - 1) & (step <= along(way) + half))
        def _():
            z_copy(way, step, h).start()

    def t_start(way, step, h):
        q = along(way)

        @pl.when((q < zl - 1) & (step <= q - half))
        def _():
            t_copy(way, step, h, False).start()

        @pl.when((q == zl - 1) & (step <= q - half))
        def _():
            t_copy(way, step, h, True).start()

    extra = max(yc // 4, 1)

    def x_copy(unit, h, less=0):
        return pltpu.make_async_remote_copy(
            src_ref=rows.at[unit, 0, pl.ds(h * piece, piece - less)],
            dst_ref=rows.at[unit, 1, pl.ds(h * piece, piece - less)],
            send_sem=x_send.at[unit, h],
            recv_sem=x_recv.at[unit, h],
            device_id=at_x(beside),
            device_id_type=MESH,
        )

    hold = half

    def x_start(way, step, h):
        near = step <= along(way)

        @pl.when(near)
        def _():
            x_copy(unit_of(way, step), h, extra * h).start()

        @pl.when(~near & (step <= along(way) + half))
        def _():
            x_copy(unit_of(way, step), h).start()

    def e_place(way, step):
        return rows.at[unit_of(way, step), 1, pl.ds(yc - extra, extra)]

    def e_copy(way, step):
        return pltpu.make_async_remote_copy(
            src_ref=e_place(way, step),
            dst_ref=e_place(way, step),
            send_sem=e_send.at[way, step],
            recv_sem=e_recv.at[way, step + 1],
            device_id=at_ring(p + (-1 if way else 1)),
            device_id_type=MESH,
        )

    def e_start(way, step):
        @pl.when((along(way) < zl - 1) & (step <= along(way)))
        def _():
            e_copy(way, step).start()

    def release():
        def early(step, carry):
            for h in range(2):
                for way in range(2):
                    x_start(way, step, h)
            return carry

        lax.fori_loop(1, hold + 1, early, 0)

    def z_round(step):
        for h in range(2):
            for way in range(2):
                @pl.when(step <= along(way) + half)
                def _():
                    place = z_place(way, step, h)
                    pltpu.make_async_copy(place, place, z_recv.at[way, step, h]).wait()

                z_start(way, step, h)

                @pl.when(step > hold)
                def _():
                    x_start(way, step, h)

                @pl.when(step <= along(way) - half)
                def _():
                    place = t_place(way, step, h)
                    pltpu.make_async_copy(place, place, t_recv.at[way, step, h]).wait()

                t_start(way, step, h)

    count = yc * MAIN

    def work(m):
        unit = unit_at(m)
        near = (m < zl) & (m > 0)

        def x_arrived(h, less):
            place = rows.at[unit, 1, pl.ds(h * piece, piece - less)]
            pltpu.make_async_copy(place, place, x_recv.at[unit, h]).wait()

        x_arrived(0, 0)

        @pl.when(near)
        def _():
            x_arrived(1, extra)

        @pl.when(~near & (m > 0))
        def _():
            x_arrived(1, 0)
        zone, s = unit // zl, unit % zl

        @pl.when(m < zl)
        def _():
            theirs = weights.at[s, pl.ds(hidden, hidden)]
            pltpu.make_async_copy(theirs, theirs, v_recv.at[s]).wait()

        w = weights[s]
        contract = (((1,), (1,)), ((), ()))
        whole = rows[unit, :, :, :, 0:width].reshape(2 * count, width)
        acc[zone, 0] += lax.dot_general(whole, w, contract, preferred_element_type=jnp.float32)
        quarters = rows[unit, :, :, :, width : width + quarter].reshape(2 * count, quarter)
        of = lax.broadcasted_iota(jnp.int32, (2 * count, quarter), 0) % MAIN // TAIL
        spread = jnp.concatenate(
            [jnp.where(of == q, quarters, jnp.zeros_like(quarters)) for q in range(4)], axis=1
        )
        acc[zone, 1] += lax.dot_general(spread, w, contract, preferred_element_type=jnp.float32)

    slots = MAIN + TAIL
    out_row = lax.broadcasted_iota(jnp.int32, (yc * slots, yc * (MAIN + 8)), 0)
    in_row = lax.broadcasted_iota(jnp.int32, (yc * slots, yc * (MAIN + 8)), 1)
    group, slot = out_row // slots, out_row % slots
    source = jnp.where(slot < MAIN, group * MAIN + slot, count + group * 8 + slot - MAIN)
    order = jnp.where(source == in_row, 1.0, 0.0).astype(jnp.bfloat16)

    def in_order(main, ends):
        ends = ends.reshape(yc, MAIN, ends.shape[-1])
        ends = (ends[:, 0:8, :] + ends[:, 8:16, :]).reshape(yc * 8, ends.shape[-1])
        ends = ends + pltpu.roll(ends, yc * 8 - TAIL, 0)
        both_parts = jnp.concatenate([main.astype(jnp.bfloat16), ends.astype(jnp.bfloat16)], axis=0)
        return jnp.dot(order, both_parts, preferred_element_type=jnp.float32)

    def s_copy(zone, col):
        return pltpu.make_async_remote_copy(
            src_ref=sums_out.at[zone, col],
            dst_ref=sums_in.at[zone, col],
            send_sem=s_send.at[zone, col],
            recv_sem=s_recv.at[zone, col],
            device_id=at_x(-beside),
            device_id_type=MESH,
        )

    def part(zone, col, cols):
        at = pl.ds(col * count, count)
        return in_order(acc[zone, 0, at, cols], acc[zone, 1, at, cols]).astype(jnp.bfloat16)

    def give(zone):
        for col in range(2):
            sums_out[zone, col] = part(zone, col, pl.ds(hidden, hidden))
            s_copy(zone, col).start()

    def store(column, zone, value):
        start = pl.multiple_of(((column + dp) % dp * 2 + zone) * yc * slots, MAIN)
        out[0, pl.ds(start, yc * slots), :] = value

    def keep(zone):
        for col in range(2):
            store(x + col * beside, zone, part(zone, col, pl.ds(0, hidden)))

    def take(zone):
        for col in range(2):
            place = sums_in.at[zone, col]
            pltpu.make_async_copy(place, place, s_recv.at[zone, col]).wait()
            store(x + (2 if col else -beside), zone, sums_in[zone, col])

    for other in range(2):
        for i in range(1, yc):
            a_copy(i, other).start()
    rows[p, 0, c] = routed[zh * yc + c]
    passing[j, c] = routed[(1 - zh) * yc + c]
    acc[...] = jnp.zeros_like(acc)
    for i in range(1, yc):
        a_arrived(i, 0)
    for h in range(2):
        for way in range(2):
            z_start(way, 0, h)
    for h in range(2):
        x_copy(p, h).start()
    for i in range(1, yc):
        a_arrived(i, 1)
    for h in range(2):
        for way in range(2):
            t_start(way, 0, h)

    late = half + 2

    def turn(r, carry):
        z_round(r + 1)

        @pl.when(r == 0)
        def _():
            place = rows.at[p, 1, pl.ds(piece, piece)]
            pltpu.make_async_copy(place, place, x_recv.at[p, 1]).wait()

        for way in range(2):
            @pl.when((r > 0) & (r <= along(way)))
            def _():
                place = e_place(way, r)
                pltpu.make_async_copy(place, place, e_recv.at[way, r]).wait()

            e_start(way, r)

        @pl.when(r + 1 == hold)
        def _():
            release()


        @pl.when(r >= late)
        def _():
            for i in range(3):
                m = 3 * (r - late) + i

                @pl.when(m < ring)
                def _():
                    work(m)

        @pl.when(r == late + (zl - 1) // 3)
        def _():
            give(zh)

        return carry

    lax.fori_loop(0, late + (ring + 2) // 3, turn, 0)
    give(1 - zh)
    keep(zh)
    take(zh)
    keep(1 - zh)
    take(1 - zh)

    for other in range(2):
        for i in range(1, yc):
            a_copy(i, other).wait_send()
    for s in range(zl):
        v_copy(s).wait_send()
    for zone in range(2):
        for col in range(2):
            s_copy(zone, col).wait_send()

    def left(step, carry):
        for way in range(2):
            q = along(way)
            for h in range(2):
                @pl.when((q < zl - 1) & (step <= q + half))
                def _():
                    z_copy(way, step, h).wait_send()

                @pl.when(step <= q - half)
                def _():
                    t_copy(way, step, h, False).wait_send()

            @pl.when((q < zl - 1) & (step <= q))
            def _():
                e_copy(way, step).wait_send()

        near = (step // zl == zh) & (step != p)
        x_copy(step, 0).wait_send()

        @pl.when(near)
        def _():
            x_copy(step, 1, extra).wait_send()

        @pl.when(~near)
        def _():
            x_copy(step, 1).wait_send()

        return carry

    lax.fori_loop(0, ring, left, 0)


def body(layer_grad, gate_probs, expert_ids, down_weight):
    dp, zl = lax.axis_size("dp"), lax.axis_size("tensor")
    experts = down_weight.shape[0] * lax.axis_size("expert")
    yc = experts // 2
    ring = 2 * zl
    width = layer_grad.shape[1]
    hidden = down_weight.shape[1]
    half = zl // 2
    chunk = (MAIN, width + width // 4)
    dma = pltpu.SemaphoreType.DMA
    steps = zl + half + 1
    vmem = pl.BlockSpec(memory_space=pltpu.VMEM)
    total = dp * experts * (MAIN + TAIL)
    return pl.pallas_call(
        functools.partial(kernel, (dp, yc, zl, width)),
        out_shape=pltpu.VMEM((1, total, hidden), jnp.bfloat16),
        in_specs=[pl.BlockSpec(memory_space=pltpu.HBM)] * 4,
        out_specs=vmem,
        scratch_shapes=[
            pltpu.VMEM(layer_grad.shape, jnp.bfloat16),
            pltpu.VMEM((2, layer_grad.shape[0]), jnp.float32),
            pltpu.VMEM((2, layer_grad.shape[0]), jnp.int32),
            dma((3,)),
            pltpu.VMEM((experts, *chunk), jnp.bfloat16),
            pltpu.VMEM((ring, 2, yc, *chunk), jnp.bfloat16),
            pltpu.VMEM((zl, yc, *chunk), jnp.bfloat16),
            pltpu.VMEM((zl, 2 * hidden, width), jnp.bfloat16),
            pltpu.VMEM((2, 2, 2 * yc * MAIN, 2 * hidden), jnp.float32),
            pltpu.VMEM((2, 2, yc * (MAIN + TAIL), hidden), jnp.bfloat16),
            pltpu.VMEM((2, 2, yc * (MAIN + TAIL), hidden), jnp.bfloat16),
            dma((zl,)),
            dma((2, yc)), dma((2, yc)),
            dma((2, steps, 2)), dma((2, steps, 2)),
            dma((2, half + 1, 2)), dma((2, half + 1, 2)),
            dma((ring, 2)), dma((ring, 2)),
            dma((zl,)), dma((zl,)),
            dma((2, 2)), dma((2, 2)),
            dma((2, zl + 1)), dma((2, zl + 1)),
        ],
        compiler_params=pltpu.CompilerParams(
            collective_id=0, has_side_effects=True, vmem_limit_bytes=56 * 1024 * 1024
        ),
        cost_estimate=pl.CostEstimate(
            flops=2 * total * hidden * width * zl,
            bytes_accessed=2 * (down_weight.size + total * hidden),
            transcendentals=0,
        ),
    )(layer_grad, gate_probs.T, expert_ids.T, down_weight)


def solution(mesh):
    placed = (
        P(("dp", "expert"), "tensor"),
        P(("dp", "expert"), None),
        P(("dp", "expert"), None),
        P("expert", ("dp", "tensor"), None),
    )
    return jax.shard_map(
        body,
        mesh=mesh,
        in_specs=placed,
        out_specs=P("expert", None, ("dp", "tensor")),
        check_vma=False,
    )
```

```python
import functools

import jax
import jax.numpy as jnp
from jax import lax
from jax.experimental import pallas as pl
from jax.experimental.pallas import tpu as pltpu
from jax.sharding import PartitionSpec as P

MESH = pl.DeviceIdType.MESH
MAIN = 16
TAIL = 4


def kernel(
    shape,
    feats_in, probs_in, ids_in, weight, out,
    feats, probs, ids, in_sem, routed, rows, passing, weights, acc, sums_out, sums_in, w_sem,
    a_send, a_recv, z_send, z_recv, t_send, t_recv, x_send, x_recv, v_send, v_recv, s_send, s_recv, e_send, e_recv,
):
    dp, yc, zl, width = shape
    half = zl // 2
    ring = 2 * zl
    quarter = width // 4
    experts = 2 * yc
    x = lax.axis_index("dp")
    ex = lax.axis_index("expert")
    j = lax.axis_index("tensor")
    zh, c = ex // yc, ex % yc
    p = zh * zl + j

    def at_ring(pos):
        pos = (pos + ring) % ring
        return {"expert": (pos // zl) * yc + c, "tensor": pos % zl}

    def at_x(offset):
        return {"dp": (x + offset + dp) % dp}

    def at_c(offset):
        return {"expert": zh * yc + (c + offset) % yc}

    loads = [
        pltpu.make_async_copy(source, target, in_sem.at[i])
        for i, (source, target) in enumerate([(ids_in, ids), (probs_in, probs), (feats_in, feats)])
    ]
    for load in loads:
        load.start()
    short, long = jnp.minimum(j, zl - 1 - j), jnp.maximum(j, zl - 1 - j)
    long_up = j > zl - 1 - j

    def unit_at(m):
        paired = m <= 2 * short
        native = m < zl
        step = jnp.where(paired, (m + 1) // 2, m - short)
        goes_up = jnp.where(paired, m % 2 == 1, long_up)
        far = m - zl
        step = jnp.where(native, step, jnp.where(far < half, short + 1 + far, long + 1 + far - half))
        goes_up = jnp.where(native, goes_up, jnp.where(far < half, ~long_up, long_up))
        return (p + jnp.where(goes_up, -step, step) + ring) % ring

    barrier = pltpu.get_barrier_semaphore()
    partners = [at_ring(p + 1), at_ring(p - 1), at_x(1), at_x(-1)] + [at_c(i) for i in range(1, yc)]
    for partner in partners:
        pl.semaphore_signal(barrier, inc=1, device_id=partner, device_id_type=MESH)

    hidden = weight.shape[1]
    w_copies = [
        pltpu.make_async_copy(
            weight.at[0, :, pl.ds(s * width, width)], weights.at[s, pl.ds(0, hidden)], w_sem.at[s]
        )
        for s in range(zl)
    ]
    for w_copy in w_copies:
        w_copy.start()

    for load in loads:
        load.wait()
    tokens = feats.shape[0]
    who = [ids[k : k + 1, :] for k in range(2)]
    e_iota = lax.broadcasted_iota(jnp.int32, (experts, tokens), 0)
    named = [(e_iota == who[k]).astype(jnp.float32) for k in range(2)]
    before = lax.broadcasted_iota(jnp.int32, (tokens, tokens), 0) < lax.broadcasted_iota(jnp.int32, (tokens, tokens), 1)
    earlier = jnp.dot(
        (named[0] + named[1]).astype(jnp.bfloat16),
        jnp.where(before, 1.0, 0.0).astype(jnp.bfloat16),
        preferred_element_type=jnp.float32,
    )
    ranks = [
        jnp.sum(earlier * named[0], axis=0, keepdims=True).astype(jnp.int32),
        jnp.sum((earlier + named[0]) * named[1], axis=0, keepdims=True).astype(jnp.int32),
    ]
    row = lax.broadcasted_iota(jnp.int32, (experts * MAIN, tokens), 0)
    sub = lax.broadcasted_iota(jnp.int32, (experts * MAIN, quarter), 0) % MAIN // TAIL

    def gather(codes, wanted):
        hits = [codes[k] == wanted for k in range(2)]
        pick = jnp.where(hits[0] | hits[1], 1.0, 0.0).astype(jnp.bfloat16)
        scale = jnp.where(hits[0], probs[0:1, :], 0.0) + jnp.where(hits[1], probs[1:2, :], 0.0)
        scale = jnp.sum(scale, axis=1, keepdims=True)
        return jnp.dot(pick, feats[...], preferred_element_type=jnp.float32), scale

    got, scale = gather([jnp.where(ranks[k] < MAIN, who[k] * MAIN + ranks[k], -1) for k in range(2)], row)
    routed[:, :, 0:width] = (got * scale).astype(jnp.bfloat16).reshape(experts, MAIN, width)
    got, scale = gather(
        [jnp.where(ranks[k] >= MAIN, who[k] * TAIL + ranks[k] - MAIN, -1) for k in range(2)],
        row // MAIN * TAIL + row % TAIL,
    )
    tail = jnp.zeros((experts * MAIN, quarter), jnp.float32)
    for q in range(4):
        tail = tail + jnp.where(sub == q, got[:, q * quarter : (q + 1) * quarter], 0.0)
    routed[:, :, width : width + quarter] = (tail * scale).astype(jnp.bfloat16).reshape(experts, MAIN, quarter)

    pl.semaphore_wait(barrier, len(partners))

    beside = jnp.where((x + c) % 2 == 0, -1, 1)

    def v_copy(s):
        return pltpu.make_async_remote_copy(
            src_ref=weights.at[s, pl.ds(0, hidden)],
            dst_ref=weights.at[s, pl.ds(hidden, hidden)],
            send_sem=v_send.at[s],
            recv_sem=v_recv.at[s],
            device_id=at_x(-beside),
            device_id_type=MESH,
        )

    def a_copy(i, other):
        target = (c + i) % yc
        source = routed.at[((1 - zh) if other else zh) * yc + target]
        return pltpu.make_async_remote_copy(
            src_ref=source,
            dst_ref=passing.at[j, c] if other else rows.at[p, 0, c],
            send_sem=a_send.at[other, i],
            recv_sem=a_recv.at[other, i],
            device_id=at_c(i),
            device_id_type=MESH,
        )

    def a_arrived(origin, other):
        @pl.when(origin != c)
        def _():
            place = passing.at[j, origin] if other else rows.at[p, 0, origin]
            pltpu.make_async_copy(place, place, a_recv.at[other, (c - origin + yc) % yc]).wait()

    piece = yc // 2

    def unit_of(way, step):
        return (p + (step if way else -step) + ring) % ring

    def along(way):
        return zl - 1 - j if way else j

    def z_place(way, step, h):
        return rows.at[unit_of(way, step), 0, pl.ds(h * piece, piece)]

    def t_place(way, step, h):
        return passing.at[(j + (step if way else -step) + zl) % zl, pl.ds(h * piece, piece)]

    def z_copy(way, step, h):
        return pltpu.make_async_remote_copy(
            src_ref=z_place(way, step, h),
            dst_ref=z_place(way, step, h),
            send_sem=z_send.at[way, step, h],
            recv_sem=z_recv.at[way, step + 1, h],
            device_id=at_ring(p + (-1 if way else 1)),
            device_id_type=MESH,
        )

    def t_copy(way, step, h, leaves):
        return pltpu.make_async_remote_copy(
            src_ref=t_place(way, step, h),
            dst_ref=(z_place if leaves else t_place)(way, step, h),
            send_sem=t_send.at[way, step, h],
            recv_sem=(z_recv if leaves else t_recv).at[way, step + 1, h],
            device_id=at_ring(p + (-1 if way else 1)),
            device_id_type=MESH,
        )

    def z_start(way, step, h):
        @pl.when((along(way) < zl - 1) & (step <= along(way) + half))
        def _():
            z_copy(way, step, h).start()

    def t_start(way, step, h):
        q = along(way)

        @pl.when((q < zl - 1) & (step <= q - half))
        def _():
            t_copy(way, step, h, False).start()

        @pl.when((q == zl - 1) & (step <= q - half))
        def _():
            t_copy(way, step, h, True).start()

    extra = max(yc // 4, 1)

    def x_copy(unit, h, less=0):
        return pltpu.make_async_remote_copy(
            src_ref=rows.at[unit, 0, pl.ds(h * piece, piece - less)],
            dst_ref=rows.at[unit, 1, pl.ds(h * piece, piece - less)],
            send_sem=x_send.at[unit, h],
            recv_sem=x_recv.at[unit, h],
            device_id=at_x(beside),
            device_id_type=MESH,
        )

    hold = half

    def x_start(way, step, h):
        near = step <= along(way)

        @pl.when(near)
        def _():
            x_copy(unit_of(way, step), h, extra * h).start()

        @pl.when(~near & (step <= along(way) + half))
        def _():
            x_copy(unit_of(way, step), h).start()

    def e_place(way, step):
        return rows.at[unit_of(way, step), 1, pl.ds(yc - extra, extra)]

    def e_copy(way, step):
        return pltpu.make_async_remote_copy(
            src_ref=e_place(way, step),
            dst_ref=e_place(way, step),
            send_sem=e_send.at[way, step],
            recv_sem=e_recv.at[way, step + 1],
            device_id=at_ring(p + (-1 if way else 1)),
            device_id_type=MESH,
        )

    def e_start(way, step):
        @pl.when((along(way) < zl - 1) & (step <= along(way)))
        def _():
            e_copy(way, step).start()

    def release():
        def early(step, carry):
            for h in range(2):
                for way in range(2):
                    x_start(way, step, h)
            return carry

        lax.fori_loop(1, hold + 1, early, 0)

    def z_round(step):
        for h in range(2):
            for way in range(2):
                @pl.when(step <= along(way) + half)
                def _():
                    place = z_place(way, step, h)
                    pltpu.make_async_copy(place, place, z_recv.at[way, step, h]).wait()

                z_start(way, step, h)

                @pl.when(step > hold)
                def _():
                    x_start(way, step, h)

                @pl.when(step <= along(way) - half)
                def _():
                    place = t_place(way, step, h)
                    pltpu.make_async_copy(place, place, t_recv.at[way, step, h]).wait()

                t_start(way, step, h)

    count = yc * MAIN

    def work(m):
        unit = unit_at(m)
        near = (m < zl) & (m > 0)

        def x_arrived(h, less):
            place = rows.at[unit, 1, pl.ds(h * piece, piece - less)]
            pltpu.make_async_copy(place, place, x_recv.at[unit, h]).wait()

        x_arrived(0, 0)

        @pl.when(near)
        def _():
            x_arrived(1, extra)

        @pl.when(~near & (m > 0))
        def _():
            x_arrived(1, 0)
        zone, s = unit // zl, unit % zl

        @pl.when(m < zl)
        def _():
            theirs = weights.at[s, pl.ds(hidden, hidden)]
            pltpu.make_async_copy(theirs, theirs, v_recv.at[s]).wait()

        w = weights[s]
        contract = (((1,), (1,)), ((), ()))
        whole = rows[unit, :, :, :, 0:width].reshape(2 * count, width)
        acc[zone, 0] += lax.dot_general(whole, w, contract, preferred_element_type=jnp.float32)
        quarters = rows[unit, :, :, :, width : width + quarter].reshape(2 * count, quarter)
        of = lax.broadcasted_iota(jnp.int32, (2 * count, quarter), 0) % MAIN // TAIL
        spread = jnp.concatenate(
            [jnp.where(of == q, quarters, jnp.zeros_like(quarters)) for q in range(4)], axis=1
        )
        acc[zone, 1] += lax.dot_general(spread, w, contract, preferred_element_type=jnp.float32)

    slots = MAIN + TAIL
    out_row = lax.broadcasted_iota(jnp.int32, (yc * slots, yc * (MAIN + 8)), 0)
    in_row = lax.broadcasted_iota(jnp.int32, (yc * slots, yc * (MAIN + 8)), 1)
    group, slot = out_row // slots, out_row % slots
    source = jnp.where(slot < MAIN, group * MAIN + slot, count + group * 8 + slot - MAIN)
    order = jnp.where(source == in_row, 1.0, 0.0).astype(jnp.bfloat16)

    def in_order(main, ends):
        ends = ends.reshape(yc, MAIN, ends.shape[-1])
        ends = (ends[:, 0:8, :] + ends[:, 8:16, :]).reshape(yc * 8, ends.shape[-1])
        ends = ends + pltpu.roll(ends, yc * 8 - TAIL, 0)
        both_parts = jnp.concatenate([main.astype(jnp.bfloat16), ends.astype(jnp.bfloat16)], axis=0)
        return jnp.dot(order, both_parts, preferred_element_type=jnp.float32)

    def s_copy(zone, col):
        return pltpu.make_async_remote_copy(
            src_ref=sums_out.at[zone, col],
            dst_ref=sums_in.at[zone, col],
            send_sem=s_send.at[zone, col],
            recv_sem=s_recv.at[zone, col],
            device_id=at_x(-beside),
            device_id_type=MESH,
        )

    def part(zone, col, cols):
        at = pl.ds(col * count, count)
        return in_order(acc[zone, 0, at, cols], acc[zone, 1, at, cols]).astype(jnp.bfloat16)

    def give(zone):
        for col in range(2):
            sums_out[zone, col] = part(zone, col, pl.ds(hidden, hidden))
            s_copy(zone, col).start()

    def store(column, zone, value):
        start = pl.multiple_of(((column + dp) % dp * 2 + zone) * yc * slots, MAIN)
        out[0, pl.ds(start, yc * slots), :] = value

    def keep(zone):
        for col in range(2):
            store(x + col * beside, zone, part(zone, col, pl.ds(0, hidden)))

    def take(zone):
        for col in range(2):
            place = sums_in.at[zone, col]
            pltpu.make_async_copy(place, place, s_recv.at[zone, col]).wait()
            store(x + (2 if col else -beside), zone, sums_in[zone, col])

    for i in range(1, yc):
        a_copy(i, 0).start()
    for s in range(zl):
        w_copies[s].wait()
    for m in range(zl):
        v_copy(unit_at(m) % zl).start()
    for i in range(1, yc):
        a_copy(i, 1).start()
    rows[p, 0, c] = routed[zh * yc + c]
    passing[j, c] = routed[(1 - zh) * yc + c]
    acc[...] = jnp.zeros_like(acc)
    for h in range(2):
        for origin in range(h * piece, (h + 1) * piece):
            a_arrived(origin, 0)
        for way in range(2):
            z_start(way, 0, h)
    for h in range(2):
        x_copy(p, h).start()
    for h in range(2):
        for origin in range(h * piece, (h + 1) * piece):
            a_arrived(origin, 1)
        for way in range(2):
            t_start(way, 0, h)

    late = half + 2

    def turn(r, carry):
        z_round(r + 1)

        @pl.when(r == 0)
        def _():
            place = rows.at[p, 1, pl.ds(piece, piece)]
            pltpu.make_async_copy(place, place, x_recv.at[p, 1]).wait()

        for way in range(2):
            @pl.when((r > 0) & (r <= along(way)))
            def _():
                place = e_place(way, r)
                pltpu.make_async_copy(place, place, e_recv.at[way, r]).wait()

            e_start(way, r)

        @pl.when(r + 1 == hold)
        def _():
            release()


        @pl.when(r >= late)
        def _():
            for i in range(3):
                m = 3 * (r - late) + i

                @pl.when(m < ring)
                def _():
                    work(m)

        @pl.when(r == late + (zl - 1) // 3)
        def _():
            give(zh)

        return carry

    lax.fori_loop(0, late + (ring + 2) // 3, turn, 0)
    give(1 - zh)
    keep(zh)
    take(zh)
    keep(1 - zh)
    take(1 - zh)

    for other in range(2):
        for i in range(1, yc):
            a_copy(i, other).wait_send()
    for s in range(zl):
        v_copy(s).wait_send()
    for zone in range(2):
        for col in range(2):
            s_copy(zone, col).wait_send()

    def left(step, carry):
        for way in range(2):
            q = along(way)
            for h in range(2):
                @pl.when((q < zl - 1) & (step <= q + half))
                def _():
                    z_copy(way, step, h).wait_send()

                @pl.when(step <= q - half)
                def _():
                    t_copy(way, step, h, False).wait_send()

            @pl.when((q < zl - 1) & (step <= q))
            def _():
                e_copy(way, step).wait_send()

        near = (step // zl == zh) & (step != p)
        x_copy(step, 0).wait_send()

        @pl.when(near)
        def _():
            x_copy(step, 1, extra).wait_send()

        @pl.when(~near)
        def _():
            x_copy(step, 1).wait_send()

        return carry

    lax.fori_loop(0, ring, left, 0)


def body(layer_grad, gate_probs, expert_ids, down_weight):
    dp, zl = lax.axis_size("dp"), lax.axis_size("tensor")
    experts = down_weight.shape[0] * lax.axis_size("expert")
    yc = experts // 2
    ring = 2 * zl
    width = layer_grad.shape[1]
    hidden = down_weight.shape[1]
    half = zl // 2
    chunk = (MAIN, width + width // 4)
    dma = pltpu.SemaphoreType.DMA
    steps = zl + half + 1
    vmem = pl.BlockSpec(memory_space=pltpu.VMEM)
    total = dp * experts * (MAIN + TAIL)
    return pl.pallas_call(
        functools.partial(kernel, (dp, yc, zl, width)),
        out_shape=pltpu.VMEM((1, total, hidden), jnp.bfloat16),
        in_specs=[pl.BlockSpec(memory_space=pltpu.HBM)] * 4,
        out_specs=vmem,
        scratch_shapes=[
            pltpu.VMEM(layer_grad.shape, jnp.bfloat16),
            pltpu.VMEM((2, layer_grad.shape[0]), jnp.float32),
            pltpu.VMEM((2, layer_grad.shape[0]), jnp.int32),
            dma((3,)),
            pltpu.VMEM((experts, *chunk), jnp.bfloat16),
            pltpu.VMEM((ring, 2, yc, *chunk), jnp.bfloat16),
            pltpu.VMEM((zl, yc, *chunk), jnp.bfloat16),
            pltpu.VMEM((zl, 2 * hidden, width), jnp.bfloat16),
            pltpu.VMEM((2, 2, 2 * yc * MAIN, 2 * hidden), jnp.float32),
            pltpu.VMEM((2, 2, yc * (MAIN + TAIL), hidden), jnp.bfloat16),
            pltpu.VMEM((2, 2, yc * (MAIN + TAIL), hidden), jnp.bfloat16),
            dma((zl,)),
            dma((2, yc)), dma((2, yc)),
            dma((2, steps, 2)), dma((2, steps, 2)),
            dma((2, half + 1, 2)), dma((2, half + 1, 2)),
            dma((ring, 2)), dma((ring, 2)),
            dma((zl,)), dma((zl,)),
            dma((2, 2)), dma((2, 2)),
            dma((2, zl + 1)), dma((2, zl + 1)),
        ],
        compiler_params=pltpu.CompilerParams(
            collective_id=0, has_side_effects=True, vmem_limit_bytes=56 * 1024 * 1024
        ),
        cost_estimate=pl.CostEstimate(
            flops=2 * total * hidden * width * zl,
            bytes_accessed=2 * (down_weight.size + total * hidden),
            transcendentals=0,
        ),
    )(layer_grad, gate_probs.T, expert_ids.T, down_weight)


def solution(mesh):
    placed = (
        P(("dp", "expert"), "tensor"),
        P(("dp", "expert"), None),
        P(("dp", "expert"), None),
        P("expert", ("dp", "tensor"), None),
    )
    return jax.shard_map(
        body,
        mesh=mesh,
        in_specs=placed,
        out_specs=P("expert", None, ("dp", "tensor")),
        check_vma=False,
    )
```

```python
import functools

import jax
import jax.numpy as jnp
from jax import lax
from jax.experimental import pallas as pl
from jax.experimental.pallas import tpu as pltpu
from jax.sharding import PartitionSpec as P

MESH = pl.DeviceIdType.MESH
MAIN = 16
TAIL = 4


def kernel(
    shape,
    feats_in, probs_in, ids_in, weight, out,
    feats, probs, ids, in_sem, routed, rows, passing, weights, acc, sums_out, sums_in, w_sem,
    a_send, a_recv, z_send, z_recv, t_send, t_recv, x_send, x_recv, v_send, v_recv, s_send, s_recv, e_send, e_recv,
):
    dp, yc, zl, width = shape
    half = zl // 2
    ring = 2 * zl
    quarter = width // 4
    experts = 2 * yc
    x = lax.axis_index("dp")
    ex = lax.axis_index("expert")
    j = lax.axis_index("tensor")
    zh, c = ex // yc, ex % yc
    p = zh * zl + j

    def at_ring(pos):
        pos = (pos + ring) % ring
        return {"expert": (pos // zl) * yc + c, "tensor": pos % zl}

    def at_x(offset):
        return {"dp": (x + offset + dp) % dp}

    def at_c(offset):
        return {"expert": zh * yc + (c + offset) % yc}

    loads = [
        pltpu.make_async_copy(source, target, in_sem.at[i])
        for i, (source, target) in enumerate([(ids_in, ids), (probs_in, probs), (feats_in, feats)])
    ]
    for load in loads:
        load.start()
    short, long = jnp.minimum(j, zl - 1 - j), jnp.maximum(j, zl - 1 - j)
    long_up = j > zl - 1 - j

    def unit_at(m):
        paired = m <= 2 * short
        native = m < zl
        step = jnp.where(paired, (m + 1) // 2, m - short)
        goes_up = jnp.where(paired, m % 2 == 1, long_up)
        far = m - zl
        step = jnp.where(native, step, jnp.where(far < half, short + 1 + far, long + 1 + far - half))
        goes_up = jnp.where(native, goes_up, jnp.where(far < half, ~long_up, long_up))
        return (p + jnp.where(goes_up, -step, step) + ring) % ring

    barrier = pltpu.get_barrier_semaphore()
    partners = [at_ring(p + 1), at_ring(p - 1), at_x(1), at_x(-1)] + [at_c(i) for i in range(1, yc)]
    for partner in partners:
        pl.semaphore_signal(barrier, inc=1, device_id=partner, device_id_type=MESH)

    hidden = weight.shape[1]
    w_copies = [
        pltpu.make_async_copy(
            weight.at[0, :, pl.ds(s * width, width)], weights.at[s, pl.ds(0, hidden)], w_sem.at[s]
        )
        for s in range(zl)
    ]
    for w_copy in w_copies:
        w_copy.start()

    for load in loads:
        load.wait()
    tokens = feats.shape[0]
    who = [ids[k : k + 1, :] for k in range(2)]
    e_iota = lax.broadcasted_iota(jnp.int32, (experts, tokens), 0)
    named = [(e_iota == who[k]).astype(jnp.float32) for k in range(2)]
    before = lax.broadcasted_iota(jnp.int32, (tokens, tokens), 0) < lax.broadcasted_iota(jnp.int32, (tokens, tokens), 1)
    earlier = jnp.dot(
        (named[0] + named[1]).astype(jnp.bfloat16),
        jnp.where(before, 1.0, 0.0).astype(jnp.bfloat16),
        preferred_element_type=jnp.float32,
    )
    ranks = [
        jnp.sum(earlier * named[0], axis=0, keepdims=True).astype(jnp.int32),
        jnp.sum((earlier + named[0]) * named[1], axis=0, keepdims=True).astype(jnp.int32),
    ]
    row = lax.broadcasted_iota(jnp.int32, (experts * MAIN, tokens), 0)
    sub = lax.broadcasted_iota(jnp.int32, (experts * MAIN, quarter), 0) % MAIN // TAIL

    def gather(codes, wanted):
        hits = [codes[k] == wanted for k in range(2)]
        pick = jnp.where(hits[0] | hits[1], 1.0, 0.0).astype(jnp.bfloat16)
        scale = jnp.where(hits[0], probs[0:1, :], 0.0) + jnp.where(hits[1], probs[1:2, :], 0.0)
        scale = jnp.sum(scale, axis=1, keepdims=True)
        return jnp.dot(pick, feats[...], preferred_element_type=jnp.float32), scale

    got, scale = gather([jnp.where(ranks[k] < MAIN, who[k] * MAIN + ranks[k], -1) for k in range(2)], row)
    routed[:, :, 0:width] = (got * scale).astype(jnp.bfloat16).reshape(experts, MAIN, width)
    got, scale = gather(
        [jnp.where(ranks[k] >= MAIN, who[k] * TAIL + ranks[k] - MAIN, -1) for k in range(2)],
        row // MAIN * TAIL + row % TAIL,
    )
    tail = jnp.zeros((experts * MAIN, quarter), jnp.float32)
    for q in range(4):
        tail = tail + jnp.where(sub == q, got[:, q * quarter : (q + 1) * quarter], 0.0)
    routed[:, :, width : width + quarter] = (tail * scale).astype(jnp.bfloat16).reshape(experts, MAIN, quarter)

    pl.semaphore_wait(barrier, len(partners))

    beside = jnp.where((x + c) % 2 == 0, -1, 1)

    def v_copy(s):
        return pltpu.make_async_remote_copy(
            src_ref=weights.at[s, pl.ds(0, hidden)],
            dst_ref=weights.at[s, pl.ds(hidden, hidden)],
            send_sem=v_send.at[s],
            recv_sem=v_recv.at[s],
            device_id=at_x(-beside),
            device_id_type=MESH,
        )

    def a_copy(i, other):
        target = (c + i) % yc
        source = routed.at[((1 - zh) if other else zh) * yc + target]
        return pltpu.make_async_remote_copy(
            src_ref=source,
            dst_ref=passing.at[j, c] if other else rows.at[p, 0, c],
            send_sem=a_send.at[other, i],
            recv_sem=a_recv.at[other, i],
            device_id=at_c(i),
            device_id_type=MESH,
        )

    def a_arrived(origin, other):
        @pl.when(origin != c)
        def _():
            place = passing.at[j, origin] if other else rows.at[p, 0, origin]
            pltpu.make_async_copy(place, place, a_recv.at[other, (c - origin + yc) % yc]).wait()

    piece = yc // 2

    def unit_of(way, step):
        return (p + (step if way else -step) + ring) % ring

    def along(way):
        return zl - 1 - j if way else j

    def z_place(way, step, h):
        return rows.at[unit_of(way, step), 0, pl.ds(h * piece, piece)]

    def t_place(way, step, h):
        return passing.at[(j + (step if way else -step) + zl) % zl, pl.ds(h * piece, piece)]

    def z_copy(way, step, h):
        return pltpu.make_async_remote_copy(
            src_ref=z_place(way, step, h),
            dst_ref=z_place(way, step, h),
            send_sem=z_send.at[way, step, h],
            recv_sem=z_recv.at[way, step + 1, h],
            device_id=at_ring(p + (-1 if way else 1)),
            device_id_type=MESH,
        )

    def t_copy(way, step, h, leaves):
        return pltpu.make_async_remote_copy(
            src_ref=t_place(way, step, h),
            dst_ref=(z_place if leaves else t_place)(way, step, h),
            send_sem=t_send.at[way, step, h],
            recv_sem=(z_recv if leaves else t_recv).at[way, step + 1, h],
            device_id=at_ring(p + (-1 if way else 1)),
            device_id_type=MESH,
        )

    def z_start(way, step, h):
        @pl.when((along(way) < zl - 1) & (step <= along(way) + half))
        def _():
            z_copy(way, step, h).start()

    def t_start(way, step, h):
        q = along(way)

        @pl.when((q < zl - 1) & (step <= q - half))
        def _():
            t_copy(way, step, h, False).start()

        @pl.when((q == zl - 1) & (step <= q - half))
        def _():
            t_copy(way, step, h, True).start()

    extra = max(yc // 4, 1)

    def x_copy(unit, h, less=0):
        return pltpu.make_async_remote_copy(
            src_ref=rows.at[unit, 0, pl.ds(h * piece, piece - less)],
            dst_ref=rows.at[unit, 1, pl.ds(h * piece, piece - less)],
            send_sem=x_send.at[unit, h],
            recv_sem=x_recv.at[unit, h],
            device_id=at_x(beside),
            device_id_type=MESH,
        )

    hold = half

    def x_start(way, step, h):
        near = step <= along(way)

        @pl.when(near)
        def _():
            x_copy(unit_of(way, step), h, extra * h).start()

        @pl.when(~near & (step <= along(way) + half))
        def _():
            x_copy(unit_of(way, step), h).start()

    def e_place(way, step):
        return rows.at[unit_of(way, step), 1, pl.ds(yc - extra, extra)]

    def e_copy(way, step):
        return pltpu.make_async_remote_copy(
            src_ref=e_place(way, step),
            dst_ref=e_place(way, step),
            send_sem=e_send.at[way, step],
            recv_sem=e_recv.at[way, step + 1],
            device_id=at_ring(p + (-1 if way else 1)),
            device_id_type=MESH,
        )

    def e_start(way, step):
        @pl.when((along(way) < zl - 1) & (step <= along(way)))
        def _():
            e_copy(way, step).start()

    def release():
        def early(step, carry):
            for h in range(2):
                for way in range(2):
                    x_start(way, step, h)
            return carry

        lax.fori_loop(1, hold + 1, early, 0)

    def z_round(step):
        for h in range(2):
            for way in range(2):
                @pl.when(step <= along(way) + half)
                def _():
                    place = z_place(way, step, h)
                    pltpu.make_async_copy(place, place, z_recv.at[way, step, h]).wait()

                z_start(way, step, h)

                @pl.when(step > hold)
                def _():
                    x_start(way, step, h)

                @pl.when(step <= along(way) - half)
                def _():
                    place = t_place(way, step, h)
                    pltpu.make_async_copy(place, place, t_recv.at[way, step, h]).wait()

                t_start(way, step, h)

    count = yc * MAIN

    def multiply(unit, first, number):
        zone, w = unit // zl, weights[unit % zl]
        contract = (((1,), (1,)), ((), ()))
        total = number * count
        at = pl.ds(first * count, total)
        whole = rows[unit, first : first + number, :, :, 0:width].reshape(total, width)
        acc[zone, 0, at] += lax.dot_general(whole, w, contract, preferred_element_type=jnp.float32)
        quarters = rows[unit, first : first + number, :, :, width : width + quarter].reshape(total, quarter)
        of = lax.broadcasted_iota(jnp.int32, (total, quarter), 0) % MAIN // TAIL
        spread = jnp.concatenate(
            [jnp.where(of == q, quarters, jnp.zeros_like(quarters)) for q in range(4)], axis=1
        )
        acc[zone, 1, at] += lax.dot_general(spread, w, contract, preferred_element_type=jnp.float32)

    def work(m):
        unit = unit_at(m)
        near = (m < zl) & (m > 0)

        def x_arrived(h, less):
            place = rows.at[unit, 1, pl.ds(h * piece, piece - less)]
            pltpu.make_async_copy(place, place, x_recv.at[unit, h]).wait()

        x_arrived(0, 0)

        @pl.when(near)
        def _():
            x_arrived(1, extra)

        @pl.when(~near & (m > 0))
        def _():
            x_arrived(1, 0)
        s = unit % zl

        @pl.when(m < zl)
        def _():
            theirs = weights.at[s, pl.ds(hidden, hidden)]
            pltpu.make_async_copy(theirs, theirs, v_recv.at[s]).wait()

        multiply(unit, 0, 2)

    slots = MAIN + TAIL
    out_row = lax.broadcasted_iota(jnp.int32, (yc * slots, yc * (MAIN + 8)), 0)
    in_row = lax.broadcasted_iota(jnp.int32, (yc * slots, yc * (MAIN + 8)), 1)
    group, slot = out_row // slots, out_row % slots
    source = jnp.where(slot < MAIN, group * MAIN + slot, count + group * 8 + slot - MAIN)
    order = jnp.where(source == in_row, 1.0, 0.0).astype(jnp.bfloat16)

    def in_order(main, ends):
        ends = ends.reshape(yc, MAIN, ends.shape[-1])
        ends = (ends[:, 0:8, :] + ends[:, 8:16, :]).reshape(yc * 8, ends.shape[-1])
        ends = ends + pltpu.roll(ends, yc * 8 - TAIL, 0)
        both_parts = jnp.concatenate([main.astype(jnp.bfloat16), ends.astype(jnp.bfloat16)], axis=0)
        return jnp.dot(order, both_parts, preferred_element_type=jnp.float32)

    def s_copy(zone, col):
        return pltpu.make_async_remote_copy(
            src_ref=sums_out.at[zone, col],
            dst_ref=sums_in.at[zone, col],
            send_sem=s_send.at[zone, col],
            recv_sem=s_recv.at[zone, col],
            device_id=at_x(-beside),
            device_id_type=MESH,
        )

    def part(zone, col, cols):
        at = pl.ds(col * count, count)
        return in_order(acc[zone, 0, at, cols], acc[zone, 1, at, cols]).astype(jnp.bfloat16)

    def give(zone, col):
        sums_out[zone, col] = part(zone, col, pl.ds(hidden, hidden))
        s_copy(zone, col).start()

    def store(column, zone, value):
        start = pl.multiple_of(((column + dp) % dp * 2 + zone) * yc * slots, MAIN)
        out[0, pl.ds(start, yc * slots), :] = value

    def keep(zone):
        for col in range(2):
            store(x + col * beside, zone, part(zone, col, pl.ds(0, hidden)))

    def take(zone):
        for col in range(2):
            place = sums_in.at[zone, col]
            pltpu.make_async_copy(place, place, s_recv.at[zone, col]).wait()
            store(x + (2 if col else -beside), zone, sums_in[zone, col])

    for i in range(1, yc):
        a_copy(i, 0).start()
    for s in range(zl):
        w_copies[s].wait()
    for m in range(zl):
        v_copy(unit_at(m) % zl).start()
    for i in range(1, yc):
        a_copy(i, 1).start()
    rows[p, 0, c] = routed[zh * yc + c]
    passing[j, c] = routed[(1 - zh) * yc + c]
    acc[...] = jnp.zeros_like(acc)
    for h in range(2):
        for origin in range(h * piece, (h + 1) * piece):
            a_arrived(origin, 0)
        for way in range(2):
            z_start(way, 0, h)
    for h in range(2):
        x_copy(p, h).start()
    for h in range(2):
        for origin in range(h * piece, (h + 1) * piece):
            a_arrived(origin, 1)
        for way in range(2):
            t_start(way, 0, h)

    late = half + 2

    def turn(r, carry):
        z_round(r + 1)

        @pl.when(r == 0)
        def _():
            place = rows.at[p, 1, pl.ds(piece, piece)]
            pltpu.make_async_copy(place, place, x_recv.at[p, 1]).wait()

        for way in range(2):
            @pl.when((r > 0) & (r <= along(way)))
            def _():
                place = e_place(way, r)
                pltpu.make_async_copy(place, place, e_recv.at[way, r]).wait()

            e_start(way, r)

        @pl.when(r + 1 == hold)
        def _():
            release()


        @pl.when(r >= late)
        def _():
            for i in range(3):
                m = 3 * (r - late) + i

                @pl.when(m < ring - 2)
                def _():
                    work(m)

        @pl.when(r == late + (zl - 1) // 3)
        def _():
            for col in range(2):
                give(zh, col)

        return carry

    lax.fori_loop(0, late + (ring + 2) // 3, turn, 0)

    last = [unit_at(ring - 2), unit_at(ring - 1)]
    for unit in last:
        multiply(unit, 0, 1)
    give(1 - zh, 0)
    for unit in last:
        for h in range(2):
            place = rows.at[unit, 1, pl.ds(h * piece, piece)]
            pltpu.make_async_copy(place, place, x_recv.at[unit, h]).wait()
        multiply(unit, 1, 1)
    give(1 - zh, 1)
    keep(zh)
    take(zh)
    keep(1 - zh)
    take(1 - zh)

    for other in range(2):
        for i in range(1, yc):
            a_copy(i, other).wait_send()
    for s in range(zl):
        v_copy(s).wait_send()
    for zone in range(2):
        for col in range(2):
            s_copy(zone, col).wait_send()

    def left(step, carry):
        for way in range(2):
            q = along(way)
            for h in range(2):
                @pl.when((q < zl - 1) & (step <= q + half))
                def _():
                    z_copy(way, step, h).wait_send()

                @pl.when(step <= q - half)
                def _():
                    t_copy(way, step, h, False).wait_send()

            @pl.when((q < zl - 1) & (step <= q))
            def _():
                e_copy(way, step).wait_send()

        near = (step // zl == zh) & (step != p)
        x_copy(step, 0).wait_send()

        @pl.when(near)
        def _():
            x_copy(step, 1, extra).wait_send()

        @pl.when(~near)
        def _():
            x_copy(step, 1).wait_send()

        return carry

    lax.fori_loop(0, ring, left, 0)


def body(layer_grad, gate_probs, expert_ids, down_weight):
    dp, zl = lax.axis_size("dp"), lax.axis_size("tensor")
    experts = down_weight.shape[0] * lax.axis_size("expert")
    yc = experts // 2
    ring = 2 * zl
    width = layer_grad.shape[1]
    hidden = down_weight.shape[1]
    half = zl // 2
    chunk = (MAIN, width + width // 4)
    dma = pltpu.SemaphoreType.DMA
    steps = zl + half + 1
    vmem = pl.BlockSpec(memory_space=pltpu.VMEM)
    total = dp * experts * (MAIN + TAIL)
    return pl.pallas_call(
        functools.partial(kernel, (dp, yc, zl, width)),
        out_shape=pltpu.VMEM((1, total, hidden), jnp.bfloat16),
        in_specs=[pl.BlockSpec(memory_space=pltpu.HBM)] * 4,
        out_specs=vmem,
        scratch_shapes=[
            pltpu.VMEM(layer_grad.shape, jnp.bfloat16),
            pltpu.VMEM((2, layer_grad.shape[0]), jnp.float32),
            pltpu.VMEM((2, layer_grad.shape[0]), jnp.int32),
            dma((3,)),
            pltpu.VMEM((experts, *chunk), jnp.bfloat16),
            pltpu.VMEM((ring, 2, yc, *chunk), jnp.bfloat16),
            pltpu.VMEM((zl, yc, *chunk), jnp.bfloat16),
            pltpu.VMEM((zl, 2 * hidden, width), jnp.bfloat16),
            pltpu.VMEM((2, 2, 2 * yc * MAIN, 2 * hidden), jnp.float32),
            pltpu.VMEM((2, 2, yc * (MAIN + TAIL), hidden), jnp.bfloat16),
            pltpu.VMEM((2, 2, yc * (MAIN + TAIL), hidden), jnp.bfloat16),
            dma((zl,)),
            dma((2, yc)), dma((2, yc)),
            dma((2, steps, 2)), dma((2, steps, 2)),
            dma((2, half + 1, 2)), dma((2, half + 1, 2)),
            dma((ring, 2)), dma((ring, 2)),
            dma((zl,)), dma((zl,)),
            dma((2, 2)), dma((2, 2)),
            dma((2, zl + 1)), dma((2, zl + 1)),
        ],
        compiler_params=pltpu.CompilerParams(
            collective_id=0, has_side_effects=True, vmem_limit_bytes=56 * 1024 * 1024
        ),
        cost_estimate=pl.CostEstimate(
            flops=2 * total * hidden * width * zl,
            bytes_accessed=2 * (down_weight.size + total * hidden),
            transcendentals=0,
        ),
    )(layer_grad, gate_probs.T, expert_ids.T, down_weight)


def solution(mesh):
    placed = (
        P(("dp", "expert"), "tensor"),
        P(("dp", "expert"), None),
        P(("dp", "expert"), None),
        P("expert", ("dp", "tensor"), None),
    )
    return jax.shard_map(
        body,
        mesh=mesh,
        in_specs=placed,
        out_specs=P("expert", None, ("dp", "tensor")),
        check_vma=False,
    )
```
